512 devices in a mesh: rows: 64 (over z, y), cols: 8 (over x, core).
Axes of the slice: x: 4, y: 4, z: 16, core: 2. Of those that a mesh axis runs over, the one named last changes fastest.
Arguments:
- tiles: float32 [12288, 128, 128], P(('rows', 'cols')), may hold values from -0.5 to 0.5
- tile_row: int32 [12288], P(('rows', 'cols')), may hold values from 0 to 255
- tile_col: int32 [12288], P(('rows', 'cols')), may hold values from 0 to 1023
- tile_counts: int32 [512], P(('rows', 'cols')), may hold values from 1 to 24, as said below
- scores: float32 [16384, 128], P('rows'), may hold values from -40 to 40
Outputs:
- weights_fit: float32 [8192, 128], P(('cols', 'rows'))
- residual: float32 [16384, 128], P('rows')
The draws below stay inside these ranges and needn't reach their ends.
Inputs may be any that keep to these rules, and one draw needn't show every extreme that they name: `tile_counts`: every device has at least one live slot, and at least one device has all 24 slots live.
All inputs are finite; a program needn't handle non-finite values.
Results may differ from the reference program's by a relative error of at most 0.0015.
Values sent between devices are 32-bit elements; how exact they have to be, the bound alone decides.
No kernel may reach another device: no remote copies, remote signals or barrier semaphores. Data moves between devices by JAX's collectives and lax.ppermute only.
A program may use at most 64 MiB of HBM per device.

```python
import math
import jax
import jax.numpy as jnp
from jax import lax

TB = 128
COLBLOCKS = 8192
RB_DEV = 256
TILE_CAP = 24
ITERS = 3
ROWBLOCKS = 16384
CB_DEV = 1024
TILES = 12288
N_ROWS = 64
N_COLS = 8


def draw_scores(key, part):
    key = jax.random.fold_in(key, 11)
    first, second = jax.random.split(key)
    position = (jnp.arange(ROWBLOCKS, dtype=jnp.float32) / ROWBLOCKS)[:, None]
    base = jax.random.truncated_normal(first, -4.0, 4.0, (ROWBLOCKS, TB), jnp.float32)
    spread = jnp.exp(jax.random.uniform(second, (ROWBLOCKS, TB), jnp.float32) * math.log(10.0))
    values = 0.3 * base * spread * (1.0 + 2.0 * position)
    return values.astype(jnp.float32)


def draw_tile_counts(key, part):
    key = jax.random.fold_in(key, 23)
    first, second, third = jax.random.split(key, 3)
    number = N_ROWS * N_COLS
    shifts = jax.random.randint(first, (number,), 0, 4)
    full = jnp.right_shift(jnp.full((number,), TILE_CAP, jnp.int32), shifts)
    jitter = jax.random.randint(second, (number,), 0, full // 4 + 1)
    counts = jnp.maximum(full - jitter, 1)
    chosen = jax.random.randint(third, (), 0, number)
    return counts.at[chosen].set(TILE_CAP).astype(jnp.int32)


def with_ends(entries, stream_key, smallest, largest):
    spot = [jax.random.randint(jax.random.fold_in(stream_key, axis), (), 0, length) for axis, length in enumerate(entries.shape)]
    main_axis = entries.shape.index(max(entries.shape))
    beside = spot[:main_axis] + [(spot[main_axis] + 1) % entries.shape[main_axis]] + spot[main_axis + 1:]
    return entries.at[tuple(spot)].set(smallest).at[tuple(beside)].set(largest)


def block_levels(rng, shape, cuts, low, top_value):
    loudness = 1.0
    for axis_at, shards_of in cuts:
        steps = jax.random.uniform(jax.random.fold_in(jax.random.fold_in(rng, 6), axis_at), (shards_of,), jnp.float32, low / len(cuts), top_value / len(cuts))
        loudness = loudness * jnp.repeat(jnp.exp(steps), shape[axis_at] // shards_of).reshape((-1,) + (1,) * (len(shape) - 1 - axis_at))
    return loudness


def centred(stream_key, dims, width, limit, cuts=(), kind=jnp.bfloat16):
    result = width * jax.random.normal(stream_key, dims, jnp.float32)
    if cuts:
        result = result * block_levels(stream_key, dims, cuts, -0.22, 0.18)
    return jnp.clip(result, -limit, limit).astype(kind)


def setup_inputs(seed: int = 0) -> dict:
    keys = jax.random.split(jax.random.key(seed), 6)
    tiles = centred(keys[0], (TILES, TB, TB), TB ** -0.5, 0.5, ((0, 512),), jnp.float32)
    tile_row = with_ends(jax.random.randint(keys[1], (TILES,), 0, RB_DEV), jax.random.fold_in(keys[1], 1), 0, RB_DEV - 1).astype(jnp.int32)
    tile_col = with_ends(jax.random.randint(keys[2], (TILES,), 0, CB_DEV), jax.random.fold_in(keys[2], 1), 0, CB_DEV - 1).astype(jnp.int32)
    tile_counts = draw_tile_counts(jax.random.fold_in(keys[5], 71), 0)
    scores = draw_scores(jax.random.fold_in(keys[5], 71), 0)
    return dict(tiles=tiles, tile_row=tile_row, tile_col=tile_col, tile_counts=tile_counts, scores=scores)


def reference(tiles, tile_row, tile_col, tile_counts, scores):
    slots = jnp.arange(TILES, dtype=jnp.int32)
    device = slots // TILE_CAP
    within = slots % TILE_CAP
    row_global = (device // N_COLS) * RB_DEV + tile_row
    col_global = (device % N_COLS) * CB_DEV + tile_col
    live = (within < tile_counts[device]).astype(jnp.float32)

    def forward(vector):
        picked = vector[col_global]
        images = jnp.einsum("tij,tj->ti", tiles, picked, precision=lax.Precision.HIGHEST) * live[:, None]
        return jax.ops.segment_sum(images, row_global, num_segments=ROWBLOCKS)

    def backward(vector):
        picked = vector[row_global]
        images = jnp.einsum("tij,ti->tj", tiles, picked, precision=lax.Precision.HIGHEST) * live[:, None]
        return jax.ops.segment_sum(images, col_global, num_segments=COLBLOCKS)

    weights_fit = jnp.zeros((COLBLOCKS, TB), jnp.float32)
    residual = scores
    gradient = backward(residual)
    norm_now = jnp.sum(gradient * gradient)
    direction = gradient
    for iteration in range(ITERS):
        image = forward(direction)
        step_size = norm_now / jnp.sum(image * image)
        weights_fit = weights_fit + step_size * direction
        residual = residual - step_size * image
        if iteration + 1 < ITERS:
            gradient = backward(residual)
            norm_next = jnp.sum(gradient * gradient)
            direction = gradient + (norm_next / norm_now) * direction
            norm_now = norm_next
    return weights_fit, residual
```

```python
import functools

import jax
import jax.numpy as jnp
from jax import lax
from jax.experimental import pallas as pl
from jax.experimental.pallas import tpu as pltpu
from jax.sharding import Mesh, PartitionSpec as P


Z, Y, X, CORE = 16, 4, 4, 2
COLS = X * CORE
ROWS = Z * Y
CAP = 24
TB = 128
ROW_BLOCKS = 256
SHARE = 16
WANT = CAP + SHARE
LINE = Z * CAP
EXTRA = 8
MSG = CAP + EXTRA
HAND = WANT + EXTRA
F32 = jnp.float32
BF16 = jnp.bfloat16


def iota(shape, dim):
    return lax.broadcasted_iota(jnp.int32, shape, dim)


def two_parts(x):
    high = x.astype(BF16).astype(F32)
    return high, x - high


def side_by_side(x):
    high, low = two_parts(x)
    return jnp.concatenate([high, low], axis=1).astype(BF16)


def picked_sum(hits, values):
    out = jnp.dot(hits, side_by_side(values), preferred_element_type=F32)
    return out[:, :TB] + out[:, TB:]


def times_tiles(vectors, split_ref, live, transposed):
    sub = iota((8, TB), 0)
    groups = []
    for g in range(CAP // 8):
        high, low = two_parts(vectors[8 * g : 8 * g + 8])
        both = jnp.concatenate([high, low], axis=0).astype(BF16)
        if transposed:
            both = jnp.concatenate([both, both], axis=1)
        total = jnp.zeros((8, TB), F32)
        for k in range(8):
            tile = split_ref[8 * g + k]
            if transposed:
                out = jnp.dot(both, tile, preferred_element_type=F32)
            else:
                out = lax.dot_general(
                    both, tile, (((1,), (1,)), ((), ())), preferred_element_type=F32
                )
                out = out[:, :TB] + out[:, TB:]
            total = jnp.where(sub == k, out[:8] + out[8:], total)
        groups.append(jnp.where(sub + 8 * g < live, total, 0.0))
    return jnp.concatenate(groups, axis=0)


def pick_rows(source, row_ref, picked):
    for j in range(CAP):
        picked[j : j + 1, :] = source[pl.ds(row_ref[j], 1), :]


def hits_of(wanted, lane_rows, width):
    pieces = [
        jnp.where(wanted == lane_rows[i : i + 1, :], 1.0, 0.0) for i in range(lane_rows.shape[0])
    ]
    return jnp.concatenate(pieces, axis=1)[:, :width].astype(BF16)


def index_rows(index_ref, live, base):
    flat = iota((EXTRA, TB), 0) * TB + iota((EXTRA, TB), 1)
    rows = jnp.zeros((EXTRA, TB), F32)
    for j in range(CAP):
        value = jnp.where(j < live, index_ref[j] + 1, 0).astype(F32)
        rows = jnp.where(flat == base + j, value, rows)
    return rows


def lane_sum(x):
    return jnp.sum(x, axis=0, keepdims=True)


def total_of(row):
    return jnp.sum(row, axis=1, keepdims=True)


def stack_rows(rows):
    sub = iota((EXTRA, TB), 0)
    out = jnp.zeros((EXTRA, TB), F32)
    for k, row in enumerate(rows):
        out = jnp.where(sub == k, row, out)
    return out


def first_kernel(row_ref, col_ref, live_ref, tiles_ref, scores_ref, out_ref, split_ref, picked):
    live = live_ref[0]
    for j in range(CAP):
        high, low = two_parts(tiles_ref[j])
        split_ref[j, :TB, :] = high.astype(BF16)
        split_ref[j, TB:, :] = low.astype(BF16)
    pick_rows(scores_ref, row_ref, picked)
    sums = times_tiles(picked[...], split_ref, live, True)
    extra = index_rows(col_ref, live, lax.axis_index("z") * CAP)
    for i in range(Z):
        out_ref[i, :CAP, :] = sums
        out_ref[i, CAP:, :] = extra


def relay_kernel(in_ref, out_ref):
    extra = in_ref[0, CAP:, :]
    for i in range(1, Z):
        extra = extra + in_ref[i, CAP:, :]
    for y in range(Y):
        for i in range(Z):
            out_ref[y, CAP * i : CAP * (i + 1), :] = in_ref[i, :CAP, :]
        out_ref[y, LINE:, :] = extra


def send_forward(vectors, split_ref, live, extra, out_ref):
    sums = times_tiles(vectors, split_ref, live, False)
    for i in range(COLS):
        out_ref[i, :CAP, :] = sums
        out_ref[i, CAP:, :] = extra


def gathered_kernel(row_ref, live_ref, in_ref, split_ref, out_ref, gradient_ref, hits_ref):
    live = live_ref[0]
    z, y = lax.axis_index("z"), lax.axis_index("y")
    lines = LINE // TB
    index = [in_ref[i, LINE : LINE + lines, :] for i in range(Y)]
    own_rows = jnp.zeros((lines, TB), F32)
    for i in range(Y):
        own_rows = jnp.where(y == i, index[i], own_rows)
    own_wanted = jnp.zeros((WANT, 1), F32)
    lane, sub = iota((CAP, TB), 1), iota((CAP, TB), 0)
    for i in range(Y):
        found = jnp.zeros((CAP, TB), F32)
        for k in range(lines):
            found = jnp.where(lane + k * TB == sub + z * CAP, index[i][k : k + 1, :], found)
        tile_part = jnp.sum(found, axis=1, keepdims=True)
        share_part = ((z * Y + i) * SHARE + 1 + iota((SHARE, 1), 0)).astype(F32)
        wanted = jnp.concatenate([tile_part, share_part], axis=0)
        hits_ref[WANT * i : WANT * (i + 1), :] = hits_of(wanted, own_rows, LINE)
        own_wanted = jnp.where(y == i, wanted, own_wanted)
    gradient = jnp.zeros((WANT, TB), F32)
    for i in range(Y):
        gradient += picked_sum(hits_of(own_wanted, index[i], LINE), in_ref[i, :LINE, :])
    gradient_ref[...] = gradient
    place = lax.axis_index("x") * CORE + lax.axis_index("core")
    extra = index_rows(row_ref, live, place * MSG)
    send_forward(gradient[:CAP], split_ref, live, extra, out_ref)


def send_backward(image_ref, row_ref, split_ref, live, scalars, out_ref, picked):
    pick_rows(image_ref, row_ref, picked)
    sums = times_tiles(picked[...], split_ref, live, True)
    extra = stack_rows(scalars)
    for i in range(Z):
        out_ref[i, :CAP, :] = sums
        out_ref[i, CAP:, :] = extra


def first_image_kernel(
    row_ref, live_ref, in_ref, split_ref, scores_ref, out_ref, image_ref, hits_ref, picked
):
    extra = in_ref[0, CAP:, :]
    for i in range(1, COLS):
        extra = extra + in_ref[i, CAP:, :]
    wanted = (iota((ROW_BLOCKS, 1), 0) + 1).astype(F32)
    hits = hits_of(wanted, extra[: COLS * MSG // TB], COLS * MSG)
    hits_ref[...] = hits
    image = picked_sum(hits, in_ref[...].reshape(COLS * MSG, TB))
    image_ref[...] = image
    scalars = [lane_sum(image * scores_ref[...]), lane_sum(image * image)]
    send_backward(image_ref, row_ref, split_ref, live_ref[0], scalars, out_ref, picked)


def hand_kernel(in_ref, hits_ref, out_ref):
    extra = in_ref[0, CAP:, :]
    for i in range(1, Z):
        extra = extra + in_ref[i, CAP:, :]
    sums = picked_sum(hits_ref[...], in_ref[:, :CAP, :].reshape(LINE, TB))
    for i in range(Y):
        out_ref[i, :WANT, :] = sums[WANT * i : WANT * (i + 1)]
        out_ref[i, WANT:, :] = extra


def added(in_ref):
    total = in_ref[0]
    for i in range(1, in_ref.shape[0]):
        total = total + in_ref[i]
    return total


def second_gradient_kernel(
    live_ref, in_ref, split_ref, gradient_ref, out_ref, product_ref, next_ref, state_ref
):
    total = added(in_ref)
    product = total[:WANT]
    norm = total_of(total[WANT : WANT + 1])
    image_norm = total_of(total[WANT + 1 : WANT + 2])
    step = norm / image_norm
    following = gradient_ref[...] - step * product
    product_ref[...] = product
    next_ref[...] = following
    state_ref[...] = stack_rows([norm, image_norm, step])
    send_forward(
        following[:CAP], split_ref, live_ref[0], jnp.zeros((EXTRA, TB), F32), out_ref
    )


def second_image_kernel(
    row_ref, live_ref, in_ref, split_ref, hits_ref, scores_ref, old_ref, state_ref,
    out_ref, image_ref, picked,
):
    image = picked_sum(hits_ref[...], in_ref[...].reshape(COLS * MSG, TB))
    image_ref[...] = image
    old = old_ref[...]
    residual = scores_ref[...] - state_ref[2:3, :] * old
    scalars = [lane_sum(image * residual), lane_sum(image * image), lane_sum(image * old)]
    send_backward(image_ref, row_ref, split_ref, live_ref[0], scalars, out_ref, picked)


def third_gradient_kernel(
    live_ref, in_ref, split_ref, first_ref, second_ref, product_ref, state_ref,
    out_ref, keep_ref, later_ref,
):
    total = added(in_ref)
    old_norm, old_image_norm, old_step = state_ref[0:1, :], state_ref[1:2, :], state_ref[2:3, :]
    norm = total_of(total[WANT : WANT + 1])
    ratio = norm / old_norm
    image_norm = (
        total_of(total[WANT + 1 : WANT + 2])
        + 2.0 * ratio * total_of(total[WANT + 2 : WANT + 3])
        + ratio * ratio * old_image_norm
    )
    step = norm / image_norm
    first, second = first_ref[...], second_ref[...]
    product = total[:WANT] + ratio * product_ref[...]
    third = second - step * product
    direction = second + ratio * first
    weights = old_step * first + step * direction
    keep_ref[0] = third[CAP:]
    keep_ref[1] = direction[CAP:]
    keep_ref[2] = weights[CAP:]
    later_ref[...] = stack_rows([norm, image_norm, step, ratio])
    send_forward(third[:CAP], split_ref, live_ref[0], jnp.zeros((EXTRA, TB), F32), out_ref)


def third_image_kernel(
    in_ref, hits_ref, scores_ref, first_ref, second_ref, state_ref, later_ref,
    out_ref, keep_ref,
):
    image = picked_sum(hits_ref[...], in_ref[...].reshape(COLS * MSG, TB))
    first = first_ref[...]
    old = second_ref[...] + later_ref[3:4, :] * first
    residual = scores_ref[...] - state_ref[2:3, :] * first - later_ref[2:3, :] * old
    keep_ref[0] = image
    keep_ref[1] = old
    keep_ref[2] = residual
    scalars = [lane_sum(image * residual), lane_sum(image * image), lane_sum(image * old)]
    extra = stack_rows(scalars)[:4]
    for i in range(ROWS):
        out_ref[i] = extra


def last_kernel(in_ref, keep_ref, image_ref, later_ref, weights_ref, residual_ref):
    total = added(in_ref)
    norm = total_of(total[0:1])
    ratio = norm / later_ref[0:1, :]
    image_norm = (
        total_of(total[1:2])
        + 2.0 * ratio * total_of(total[2:3])
        + ratio * ratio * later_ref[1:2, :]
    )
    step = norm / image_norm
    weights_ref[...] = keep_ref[2] + step * (keep_ref[0] + ratio * keep_ref[1])
    residual_ref[...] = image_ref[2] - step * (image_ref[0] + ratio * image_ref[1])


def call(kernel, outs, args, picked=False):
    def spec(x):
        scalar = x.dtype == jnp.int32
        return pl.BlockSpec(memory_space=pltpu.SMEM if scalar else pltpu.VMEM)

    return pl.pallas_call(
        kernel,
        out_shape=[jax.ShapeDtypeStruct(s, d) for s, d in outs],
        in_specs=[spec(a) for a in args],
        out_specs=[pl.BlockSpec(memory_space=pltpu.VMEM) for _ in outs],
        scratch_shapes=[pltpu.VMEM((CAP, TB), F32)] if picked else [],
        compiler_params=pltpu.CompilerParams(vmem_limit_bytes=16 * 2**20),
        name=kernel.__name__,
    )(*args)


def swap(x, axes):
    return lax.all_to_all(x, axes, 0, 0, tiled=True)


def local(tiles, tile_row, tile_col, tile_counts, scores):
    f = lambda *shape: (shape, F32)
    b = lambda *shape: (shape, BF16)
    cols = ("x", "core")
    to_z, to_y = f(Z, MSG, TB), f(Y, HAND, TB)
    to_cols = f(COLS, MSG, TB)
    image_shape, state_shape = f(ROW_BLOCKS, TB), f(EXTRA, TB)

    message, split = call(
        first_kernel,
        [to_z, b(CAP, 2 * TB, TB)],
        [tile_row, tile_col, tile_counts, tiles, scores],
        True,
    )
    (message,) = call(relay_kernel, [f(Y, LINE + EXTRA, TB)], [swap(message, "z")])
    message, first, hand_hits = call(
        gathered_kernel,
        [to_cols, f(WANT, TB), b(Y * WANT, LINE)],
        [tile_row, tile_counts, swap(message, "y"), split],
    )
    message, image, row_hits = call(
        first_image_kernel,
        [to_z, image_shape, b(ROW_BLOCKS, COLS * MSG)],
        [tile_row, tile_counts, swap(message, cols), split, scores],
        True,
    )
    (message,) = call(hand_kernel, [to_y], [swap(message, "z"), hand_hits])
    message, product, second, state = call(
        second_gradient_kernel,
        [to_cols, f(WANT, TB), f(WANT, TB), state_shape],
        [tile_counts, swap(message, "y"), split, first],
    )
    message, second_image = call(
        second_image_kernel,
        [to_z, image_shape],
        [tile_row, tile_counts, swap(message, cols), split, row_hits, scores, image, state],
        True,
    )
    (message,) = call(hand_kernel, [to_y], [swap(message, "z"), hand_hits])
    message, keep, later = call(
        third_gradient_kernel,
        [to_cols, f(3, SHARE, TB), state_shape],
        [tile_counts, swap(message, "y"), split, first, second, product, state],
    )
    message, images = call(
        third_image_kernel,
        [f(ROWS, 4, TB), f(3, ROW_BLOCKS, TB)],
        [swap(message, cols), row_hits, scores, image, second_image, state, later],
    )
    weights, residual = call(
        last_kernel,
        [f(SHARE, TB), image_shape],
        [swap(message, ("z", "y")), keep, images, later],
    )
    return weights, residual


def solution(mesh):
    fine = Mesh(mesh.devices.reshape(Z, Y, X, CORE), ("z", "y", "x", "core"))
    every = ("z", "y", "x", "core")
    return jax.shard_map(
        local,
        mesh=fine,
        in_specs=(P(every, None, None), P(every), P(every), P(every), P(("z", "y"), None)),
        out_specs=(P(("x", "core", "z", "y"), None), P(("z", "y"), None)),
        check_vma=False,
    )
```

```python
import functools

import jax
import jax.numpy as jnp
from jax import lax
from jax.experimental import pallas as pl
from jax.experimental.pallas import tpu as pltpu
from jax.sharding import Mesh, PartitionSpec as P


Z, Y, X, CORE = 16, 4, 4, 2
COLS = X * CORE
ROWS = Z * Y
CAP = 24
TB = 128
ROW_BLOCKS = 256
SHARE = 16
WANT = CAP + SHARE
EXTRA = 8
MSG = CAP + 1
LINE = Z * MSG
SIDE = COLS * MSG
HAND = WANT + EXTRA
PARTS = 3
F32 = jnp.float32
BF16 = jnp.bfloat16


def iota(shape, dim):
    return lax.broadcasted_iota(jnp.int32, shape, dim)


def two_parts(x):
    high = x.astype(BF16).astype(F32)
    return high, x - high


def side_by_side(x):
    high, low = two_parts(x)
    return jnp.concatenate([high, low], axis=1).astype(BF16)


def picked_sum(hits, values):
    out = jnp.dot(hits, side_by_side(values), preferred_element_type=F32)
    return out[:, :TB] + out[:, TB:]


def times_tiles(vectors, split_ref, live, transposed):
    sub = iota((8, TB), 0)
    groups = []
    for g in range(CAP // 8):
        high, low = two_parts(vectors[8 * g : 8 * g + 8])
        both = jnp.concatenate([high, low], axis=0).astype(BF16)
        if transposed:
            both = jnp.concatenate([both, both], axis=1)
        total = jnp.zeros((8, TB), F32)
        for k in range(8):
            tile = split_ref[8 * g + k]
            if transposed:
                out = jnp.dot(both, tile, preferred_element_type=F32)
            else:
                out = lax.dot_general(
                    both, tile, (((1,), (1,)), ((), ())), preferred_element_type=F32
                )
                out = out[:, :TB] + out[:, TB:]
            total = jnp.where(sub == k, out[:8] + out[8:], total)
        groups.append(jnp.where(sub + 8 * g < live, total, 0.0))
    return jnp.concatenate(groups, axis=0)


def pick_rows(source, row_ref, picked):
    for j in range(CAP):
        picked[j : j + 1, :] = source[pl.ds(row_ref[j], 1), :]


def hits_of(wanted, lane_rows, width):
    pieces = [jnp.where(wanted == row, 1.0, 0.0) for row in lane_rows]
    return jnp.concatenate(pieces, axis=1)[:, :width].astype(BF16)


def index_row(index_ref, live, base):
    lane = iota((1, TB), 1)
    row = jnp.zeros((1, TB), F32)
    for j in range(CAP):
        value = jnp.where(j < live, index_ref[j] + 1, 0).astype(F32)
        row = jnp.where(lane == lax.rem(base + j, TB), value, row)
    return row


def index_lanes(in_ref, count):
    lane = iota((1, TB), 1)
    rows = []
    for k in range(-(-count * MSG // TB)):
        row = jnp.zeros((1, TB), F32)
        for i in range(count):
            low, high = MSG * i - TB * k, MSG * i + CAP - TB * k
            if high > 0 and low < TB:
                mine = (lane >= low) & (lane < high)
                row = jnp.where(mine, in_ref[MSG * i + CAP : MSG * (i + 1), :], row)
        rows.append(row)
    return rows


def send_to_all(out_ref, count, sums, row):
    message = jnp.concatenate([sums, row], axis=0)
    for i in range(count):
        out_ref[MSG * i : MSG * (i + 1), :] = message


def extra_sum(in_ref, count):
    row = in_ref[CAP : CAP + 1, :]
    for i in range(1, count):
        row = row + in_ref[MSG * i + CAP : MSG * (i + 1), :]
    return row


def scalar_row(rows):
    sums = jnp.sum(stack_rows(rows), axis=1, keepdims=True)
    apart = jnp.where(iota((EXTRA, TB), 0) == iota((EXTRA, TB), 1), sums, 0.0)
    return jnp.sum(apart, axis=0, keepdims=True)


def scalars_of(row, count):
    apart = jnp.where(iota((EXTRA, TB), 0) == iota((EXTRA, TB), 1), row, 0.0)
    sums = jnp.sum(apart, axis=1, keepdims=True)
    return [sums[k : k + 1] for k in range(count)]


def lane_sum(x):
    return jnp.sum(x, axis=0, keepdims=True)


def stack_rows(rows):
    sub = iota((EXTRA, TB), 0)
    out = jnp.zeros((EXTRA, TB), F32)
    for k, row in enumerate(rows):
        out = jnp.where(sub == k, row, out)
    return out


def first_kernel(
    row_hbm, col_hbm, live_hbm, tiles_hbm, scores_hbm, out_ref, split_ref,
    row_ref, col_ref, live_ref, tiles, scores, picked, done,
):
    part = CAP // PARTS
    copies = [
        pltpu.make_async_copy(row_hbm, row_ref, done.at[0]),
        pltpu.make_async_copy(col_hbm, col_ref, done.at[1]),
        pltpu.make_async_copy(live_hbm, live_ref, done.at[2]),
        pltpu.make_async_copy(scores_hbm, scores, done.at[3]),
    ]
    for i in range(PARTS):
        some = pl.ds(part * i, part)
        copies.append(pltpu.make_async_copy(tiles_hbm.at[some], tiles.at[some], done.at[4 + i]))
    for copy in copies:
        copy.start()
    for copy in copies[:4]:
        copy.wait()
    live = live_ref[0]
    pick_rows(scores, row_ref, picked)
    row = index_row(col_ref, live, lax.axis_index("z") * MSG)
    for i in range(PARTS):
        copies[4 + i].wait()
        for j in range(part * i, part * (i + 1)):
            high, low = two_parts(tiles[j])
            split_ref[j, :TB, :] = high.astype(BF16)
            split_ref[j, TB:, :] = low.astype(BF16)
    sums = times_tiles(picked[...], split_ref, live, True)
    send_to_all(out_ref, Z, sums, row)


def relay_kernel(in_ref, out_ref):
    rows = index_lanes(in_ref, Z)
    for y in range(Y):
        out_ref[y, :LINE, :] = in_ref[...]
        out_ref[y, LINE:, :] = stack_rows(rows)


def send_forward(vectors, split_ref, live, row, out_ref):
    send_to_all(out_ref, COLS, times_tiles(vectors, split_ref, live, False), row)


def gathered_kernel(row_ref, live_ref, in_ref, split_ref, out_ref, gradient_ref, hits_ref):
    live = live_ref[0]
    z, y = lax.axis_index("z"), lax.axis_index("y")
    lines = -(-LINE // TB)
    index = [[in_ref[i, LINE + k : LINE + k + 1, :] for k in range(lines)] for i in range(Y)]
    own_rows = index[0]
    for i in range(1, Y):
        own_rows = [jnp.where(y == i, new, old) for new, old in zip(index[i], own_rows)]
    own_wanted = jnp.zeros((WANT, 1), F32)
    lane, sub = iota((CAP, TB), 1), iota((CAP, TB), 0)
    for i in range(Y):
        found = jnp.zeros((CAP, TB), F32)
        for k in range(lines):
            found = jnp.where(lane + k * TB == sub + z * MSG, index[i][k], found)
        tile_part = jnp.sum(found, axis=1, keepdims=True)
        share_part = ((z * Y + i) * SHARE + 1 + iota((SHARE, 1), 0)).astype(F32)
        wanted = jnp.concatenate([tile_part, share_part], axis=0)
        hits_ref[WANT * i : WANT * (i + 1), :] = hits_of(wanted, own_rows, LINE)
        own_wanted = jnp.where(y == i, wanted, own_wanted)
    gradient = jnp.zeros((WANT, TB), F32)
    for i in range(Y):
        gradient += picked_sum(hits_of(own_wanted, index[i], LINE), in_ref[i, :LINE, :])
    gradient_ref[...] = gradient
    place = lax.axis_index("x") * CORE + lax.axis_index("core")
    row = index_row(row_ref, live, place * MSG)
    send_forward(gradient[:CAP], split_ref, live, row, out_ref)


def send_backward(image_ref, row_ref, split_ref, live, scalars, out_ref, picked):
    pick_rows(image_ref, row_ref, picked)
    sums = times_tiles(picked[...], split_ref, live, True)
    send_to_all(out_ref, Z, sums, scalar_row(scalars))


def first_image_kernel(
    row_ref, live_ref, in_ref, split_ref, scores_ref, out_ref, image_ref, hits_ref, picked
):
    wanted = (iota((ROW_BLOCKS, 1), 0) + 1).astype(F32)
    hits = hits_of(wanted, index_lanes(in_ref, COLS), SIDE)
    hits_ref[...] = hits
    image = picked_sum(hits, in_ref[...])
    image_ref[...] = image
    scalars = [lane_sum(image * scores_ref[...]), lane_sum(image * image)]
    send_backward(image_ref, row_ref, split_ref, live_ref[0], scalars, out_ref, picked)


def hand_kernel(in_ref, hits_ref, out_ref):
    extra = jnp.broadcast_to(extra_sum(in_ref, Z), (EXTRA, TB))
    sums = picked_sum(hits_ref[...], in_ref[...])
    for i in range(Y):
        out_ref[i, :WANT, :] = sums[WANT * i : WANT * (i + 1)]
        out_ref[i, WANT:, :] = extra


def added(in_ref):
    total = in_ref[0]
    for i in range(1, in_ref.shape[0]):
        total = total + in_ref[i]
    return total


def second_gradient_kernel(
    live_ref, in_ref, split_ref, gradient_ref, out_ref, product_ref, next_ref, state_ref
):
    total = added(in_ref)
    product = total[:WANT]
    norm, image_norm = scalars_of(total[WANT : WANT + 1], 2)
    step = norm / image_norm
    following = gradient_ref[...] - step * product
    product_ref[...] = product
    next_ref[...] = following
    state_ref[...] = stack_rows([norm, image_norm, step])
    send_forward(
        following[:CAP], split_ref, live_ref[0], jnp.zeros((1, TB), F32), out_ref
    )


def second_image_kernel(
    row_ref, live_ref, in_ref, split_ref, hits_ref, scores_ref, old_ref, state_ref,
    out_ref, image_ref, picked,
):
    image = picked_sum(hits_ref[...], in_ref[...])
    image_ref[...] = image
    old = old_ref[...]
    residual = scores_ref[...] - state_ref[2:3, :] * old
    scalars = [lane_sum(image * residual), lane_sum(image * image), lane_sum(image * old)]
    send_backward(image_ref, row_ref, split_ref, live_ref[0], scalars, out_ref, picked)


def third_gradient_kernel(
    live_ref, in_ref, split_ref, first_ref, second_ref, product_ref, state_ref,
    out_ref, keep_ref, later_ref,
):
    total = added(in_ref)
    old_norm, old_image_norm, old_step = state_ref[0:1, :], state_ref[1:2, :], state_ref[2:3, :]
    norm, straight, cross = scalars_of(total[WANT : WANT + 1], 3)
    ratio = norm / old_norm
    image_norm = straight + 2.0 * ratio * cross + ratio * ratio * old_image_norm
    step = norm / image_norm
    first, second = first_ref[...], second_ref[...]
    product = total[:WANT] + ratio * product_ref[...]
    third = second - step * product
    direction = second + ratio * first
    weights = old_step * first + step * direction
    keep_ref[0] = third[CAP:]
    keep_ref[1] = direction[CAP:]
    keep_ref[2] = weights[CAP:]
    later_ref[...] = stack_rows([norm, image_norm, step, ratio])
    send_forward(third[:CAP], split_ref, live_ref[0], jnp.zeros((1, TB), F32), out_ref)


def third_image_kernel(
    in_ref, hits_ref, scores_ref, first_ref, second_ref, state_ref, later_ref,
    out_ref, keep_ref,
):
    image = picked_sum(hits_ref[...], in_ref[...])
    first = first_ref[...]
    old = second_ref[...] + later_ref[3:4, :] * first
    residual = scores_ref[...] - state_ref[2:3, :] * first - later_ref[2:3, :] * old
    keep_ref[0] = image
    keep_ref[1] = old
    keep_ref[2] = residual
    scalars = [lane_sum(image * residual), lane_sum(image * image), lane_sum(image * old)]
    out_ref[...] = jnp.broadcast_to(scalar_row(scalars), (ROWS, TB))


def last_kernel(in_ref, keep_ref, image_ref, later_ref, weights_ref, residual_ref):
    norm, straight, cross = scalars_of(lane_sum(in_ref[...]), 3)
    ratio = norm / later_ref[0:1, :]
    image_norm = straight + 2.0 * ratio * cross + ratio * ratio * later_ref[1:2, :]
    step = norm / image_norm
    weights_ref[...] = keep_ref[2] + step * (keep_ref[0] + ratio * keep_ref[1])
    residual_ref[...] = image_ref[2] - step * (image_ref[0] + ratio * image_ref[1])


def call(kernel, outs, args, scratch=(), memory=None, room=16 * 2**20):
    def spec(x):
        scalar = x.dtype == jnp.int32
        return pl.BlockSpec(memory_space=memory or (pltpu.SMEM if scalar else pltpu.VMEM))

    return pl.pallas_call(
        kernel,
        out_shape=[jax.ShapeDtypeStruct(s, d) for s, d in outs],
        in_specs=[spec(a) for a in args],
        out_specs=[pl.BlockSpec(memory_space=pltpu.VMEM) for _ in outs],
        scratch_shapes=list(scratch),
        compiler_params=pltpu.CompilerParams(vmem_limit_bytes=room),
        name=kernel.__name__,
    )(*args)


def swap(x, axes, count):
    shape = x.shape
    if len(shape) == 2:
        x = x.reshape(count, shape[0] // count, 1, TB)
    return lax.all_to_all(x, axes, 0, 0, tiled=True).reshape(shape)


def local(tiles, tile_row, tile_col, tile_counts, scores):
    f = lambda *shape: (shape, F32)
    b = lambda *shape: (shape, BF16)
    cols = ("x", "core")
    to_z, to_y = f(LINE, TB), f(Y, HAND, TB)
    to_cols = f(SIDE, TB)
    image_shape, state_shape = f(ROW_BLOCKS, TB), f(EXTRA, TB)
    picked = [pltpu.VMEM((CAP, TB), F32)]

    message, split = call(
        first_kernel,
        [to_z, b(CAP, 2 * TB, TB)],
        [tile_row, tile_col, tile_counts, tiles, scores],
        [
            pltpu.SMEM((CAP,), jnp.int32),
            pltpu.SMEM((CAP,), jnp.int32),
            pltpu.SMEM((1,), jnp.int32),
            pltpu.VMEM((CAP, TB, TB), F32),
            pltpu.VMEM((ROW_BLOCKS, TB), F32),
            *picked,
            pltpu.SemaphoreType.DMA((4 + PARTS,)),
        ],
        pltpu.HBM,
        62 * 2**20,
    )
    (message,) = call(relay_kernel, [f(Y, LINE + EXTRA, TB)], [swap(message, "z", Z)])
    message, first, hand_hits = call(
        gathered_kernel,
        [to_cols, f(WANT, TB), b(Y * WANT, LINE)],
        [tile_row, tile_counts, swap(message, "y", Y), split],
    )
    message, image, row_hits = call(
        first_image_kernel,
        [to_z, image_shape, b(ROW_BLOCKS, SIDE)],
        [tile_row, tile_counts, swap(message, cols, COLS), split, scores],
        picked,
    )
    (message,) = call(hand_kernel, [to_y], [swap(message, "z", Z), hand_hits])
    message, product, second, state = call(
        second_gradient_kernel,
        [to_cols, f(WANT, TB), f(WANT, TB), state_shape],
        [tile_counts, swap(message, "y", Y), split, first],
    )
    message, second_image = call(
        second_image_kernel,
        [to_z, image_shape],
        [tile_row, tile_counts, swap(message, cols, COLS), split, row_hits, scores, image, state],
        picked,
    )
    (message,) = call(hand_kernel, [to_y], [swap(message, "z", Z), hand_hits])
    message, keep, later = call(
        third_gradient_kernel,
        [to_cols, f(3, SHARE, TB), state_shape],
        [tile_counts, swap(message, "y", Y), split, first, second, product, state],
    )
    message, images = call(
        third_image_kernel,
        [f(ROWS, TB), f(3, ROW_BLOCKS, TB)],
        [swap(message, cols, COLS), row_hits, scores, image, second_image, state, later],
    )
    weights, residual = call(
        last_kernel,
        [f(SHARE, TB), image_shape],
        [swap(message, ("z", "y"), ROWS), keep, images, later],
    )
    return weights, residual


def solution(mesh):
    fine = Mesh(mesh.devices.reshape(Z, Y, X, CORE), ("z", "y", "x", "core"))
    every = ("z", "y", "x", "core")
    return jax.shard_map(
        local,
        mesh=fine,
        in_specs=(P(every, None, None), P(every), P(every), P(every), P(("z", "y"), None)),
        out_specs=(P(("x", "core", "z", "y"), None), P(("z", "y"), None)),
        check_vma=False,
    )
```

```python
import functools

import jax
import jax.numpy as jnp
from jax import lax
from jax.experimental import pallas as pl
from jax.experimental.pallas import tpu as pltpu
from jax.sharding import Mesh, PartitionSpec as P


FAR, PAIR, Y, X, CORE = 8, 2, 4, 4, 2
NEAR = PAIR * Y
COLS = X * CORE
ROWS = FAR * NEAR
CAP = 24
TB = 128
ROW_BLOCKS = 256
SHARE = 16
WANT = CAP + SHARE
EXTRA = 8
MSG = CAP + 1
LINE = FAR * MSG
SIDE = COLS * MSG
HAND = WANT + EXTRA
PARTS = 3
F32 = jnp.float32
BF16 = jnp.bfloat16


def iota(shape, dim):
    return lax.broadcasted_iota(jnp.int32, shape, dim)


def two_parts(x):
    high = x.astype(BF16).astype(F32)
    return high, x - high


def side_by_side(x):
    high, low = two_parts(x)
    return jnp.concatenate([high, low], axis=1).astype(BF16)


def picked_sum(hits, values):
    out = jnp.dot(hits, side_by_side(values), preferred_element_type=F32)
    return out[:, :TB] + out[:, TB:]


def times_tiles(vectors, split_ref, live, transposed):
    sub = iota((8, TB), 0)
    groups = []
    for g in range(CAP // 8):
        high, low = two_parts(vectors[8 * g : 8 * g + 8])
        both = jnp.concatenate([high, low], axis=0).astype(BF16)
        if transposed:
            both = jnp.concatenate([both, both], axis=1)
        total = jnp.zeros((8, TB), F32)
        for k in range(8):
            tile = split_ref[8 * g + k]
            if transposed:
                out = jnp.dot(both, tile, preferred_element_type=F32)
            else:
                out = lax.dot_general(
                    both, tile, (((1,), (1,)), ((), ())), preferred_element_type=F32
                )
                out = out[:, :TB] + out[:, TB:]
            total = jnp.where(sub == k, out[:8] + out[8:], total)
        groups.append(jnp.where(sub + 8 * g < live, total, 0.0))
    return jnp.concatenate(groups, axis=0)


def pick_rows(source, row_ref, picked):
    for j in range(CAP):
        picked[j : j + 1, :] = source[pl.ds(row_ref[j], 1), :]


def hits_of(wanted, lane_rows, width):
    pieces = [jnp.where(wanted == row, 1.0, 0.0) for row in lane_rows]
    return jnp.concatenate(pieces, axis=1)[:, :width].astype(BF16)


def index_row(index_ref, live, base):
    lane = iota((1, TB), 1)
    row = jnp.zeros((1, TB), F32)
    for j in range(CAP):
        value = jnp.where(j < live, index_ref[j] + 1, 0).astype(F32)
        row = jnp.where(lane == lax.rem(base + j, TB), value, row)
    return row


def index_lanes(in_ref, count):
    lane = iota((1, TB), 1)
    rows = []
    for k in range(-(-count * MSG // TB)):
        row = jnp.zeros((1, TB), F32)
        for i in range(count):
            low, high = MSG * i - TB * k, MSG * i + CAP - TB * k
            if high > 0 and low < TB:
                mine = (lane >= low) & (lane < high)
                row = jnp.where(mine, in_ref[MSG * i + CAP : MSG * (i + 1), :], row)
        rows.append(row)
    return rows


def send_to_all(out_ref, count, sums, row):
    message = jnp.concatenate([sums, row], axis=0)
    for i in range(count):
        out_ref[MSG * i : MSG * (i + 1), :] = message


def extra_sum(in_ref, count):
    row = in_ref[CAP : CAP + 1, :]
    for i in range(1, count):
        row = row + in_ref[MSG * i + CAP : MSG * (i + 1), :]
    return row


def scalar_row(rows):
    sums = jnp.sum(stack_rows(rows), axis=1, keepdims=True)
    apart = jnp.where(iota((EXTRA, TB), 0) == iota((EXTRA, TB), 1), sums, 0.0)
    return jnp.sum(apart, axis=0, keepdims=True)


def scalars_of(row, count):
    apart = jnp.where(iota((EXTRA, TB), 0) == iota((EXTRA, TB), 1), row, 0.0)
    sums = jnp.sum(apart, axis=1, keepdims=True)
    return [sums[k : k + 1] for k in range(count)]


def lane_sum(x):
    return jnp.sum(x, axis=0, keepdims=True)


def stack_rows(rows):
    sub = iota((EXTRA, TB), 0)
    out = jnp.zeros((EXTRA, TB), F32)
    for k, row in enumerate(rows):
        out = jnp.where(sub == k, row, out)
    return out


def first_kernel(
    row_hbm, col_hbm, live_hbm, tiles_hbm, scores_hbm, out_ref, split_ref,
    row_ref, col_ref, live_ref, tiles, scores, picked, done,
):
    part = CAP // PARTS
    copies = [
        pltpu.make_async_copy(row_hbm, row_ref, done.at[0]),
        pltpu.make_async_copy(col_hbm, col_ref, done.at[1]),
        pltpu.make_async_copy(live_hbm, live_ref, done.at[2]),
        pltpu.make_async_copy(scores_hbm, scores, done.at[3]),
    ]
    for i in range(PARTS):
        some = pl.ds(part * i, part)
        copies.append(pltpu.make_async_copy(tiles_hbm.at[some], tiles.at[some], done.at[4 + i]))
    for copy in copies:
        copy.start()
    for copy in copies[:4]:
        copy.wait()
    live = live_ref[0]
    pick_rows(scores, row_ref, picked)
    row = index_row(col_ref, live, lax.axis_index("far") * MSG)
    for i in range(PARTS):
        copies[4 + i].wait()
        for j in range(part * i, part * (i + 1)):
            high, low = two_parts(tiles[j])
            split_ref[j, :TB, :] = high.astype(BF16)
            split_ref[j, TB:, :] = low.astype(BF16)
    sums = times_tiles(picked[...], split_ref, live, True)
    send_to_all(out_ref, FAR, sums, row)


def relay_kernel(in_ref, out_ref):
    rows = index_lanes(in_ref, FAR)
    for i in range(NEAR):
        out_ref[i, :LINE, :] = in_ref[...]
        out_ref[i, LINE:, :] = stack_rows(rows)


def send_forward(vectors, split_ref, live, row, out_ref):
    send_to_all(out_ref, COLS, times_tiles(vectors, split_ref, live, False), row)


def gathered_kernel(row_ref, live_ref, in_ref, split_ref, out_ref, gradient_ref, hits_ref):
    live = live_ref[0]
    far = lax.axis_index("far")
    near = lax.axis_index("pair") * Y + lax.axis_index("y")
    lines = -(-LINE // TB)
    index = [[in_ref[i, LINE + k : LINE + k + 1, :] for k in range(lines)] for i in range(NEAR)]
    own_rows = index[0]
    for i in range(1, NEAR):
        own_rows = [jnp.where(near == i, new, old) for new, old in zip(index[i], own_rows)]
    own_wanted = jnp.zeros((WANT, 1), F32)
    lane, sub = iota((CAP, TB), 1), iota((CAP, TB), 0)
    for i in range(NEAR):
        found = jnp.zeros((CAP, TB), F32)
        for k in range(lines):
            found = jnp.where(lane + k * TB == sub + far * MSG, index[i][k], found)
        tile_part = jnp.sum(found, axis=1, keepdims=True)
        share_part = ((far * NEAR + i) * SHARE + 1 + iota((SHARE, 1), 0)).astype(F32)
        wanted = jnp.concatenate([tile_part, share_part], axis=0)
        hits_ref[WANT * i : WANT * (i + 1), :] = hits_of(wanted, own_rows, LINE)
        own_wanted = jnp.where(near == i, wanted, own_wanted)
    gradient = jnp.zeros((WANT, TB), F32)
    for i in range(NEAR):
        gradient += picked_sum(hits_of(own_wanted, index[i], LINE), in_ref[i, :LINE, :])
    gradient_ref[...] = gradient
    place = lax.axis_index("x") * CORE + lax.axis_index("core")
    row = index_row(row_ref, live, place * MSG)
    send_forward(gradient[:CAP], split_ref, live, row, out_ref)


def send_backward(image_ref, row_ref, split_ref, live, scalars, out_ref, picked):
    pick_rows(image_ref, row_ref, picked)
    sums = times_tiles(picked[...], split_ref, live, True)
    send_to_all(out_ref, FAR, sums, scalar_row(scalars))


def first_image_kernel(
    row_ref, live_ref, in_ref, split_ref, scores_ref, out_ref, image_ref, hits_ref, picked
):
    wanted = (iota((ROW_BLOCKS, 1), 0) + 1).astype(F32)
    hits = hits_of(wanted, index_lanes(in_ref, COLS), SIDE)
    hits_ref[...] = hits
    image = picked_sum(hits, in_ref[...])
    image_ref[...] = image
    scalars = [lane_sum(image * scores_ref[...]), lane_sum(image * image)]
    send_backward(image_ref, row_ref, split_ref, live_ref[0], scalars, out_ref, picked)


def hand_kernel(in_ref, hits_ref, out_ref):
    extra = jnp.broadcast_to(extra_sum(in_ref, FAR), (EXTRA, TB))
    sums = picked_sum(hits_ref[...], in_ref[...])
    for i in range(NEAR):
        out_ref[i, :WANT, :] = sums[WANT * i : WANT * (i + 1)]
        out_ref[i, WANT:, :] = extra


def added(in_ref):
    total = in_ref[0]
    for i in range(1, in_ref.shape[0]):
        total = total + in_ref[i]
    return total


def second_gradient_kernel(
    live_ref, in_ref, split_ref, gradient_ref, out_ref, product_ref, next_ref, state_ref
):
    total = added(in_ref)
    product = total[:WANT]
    norm, image_norm = scalars_of(total[WANT : WANT + 1], 2)
    step = norm / image_norm
    following = gradient_ref[...] - step * product
    product_ref[...] = product
    next_ref[...] = following
    state_ref[...] = stack_rows([norm, image_norm, step])
    send_forward(
        following[:CAP], split_ref, live_ref[0], jnp.zeros((1, TB), F32), out_ref
    )


def second_image_kernel(
    row_ref, live_ref, in_ref, split_ref, hits_ref, scores_ref, old_ref, state_ref,
    out_ref, image_ref, picked,
):
    image = picked_sum(hits_ref[...], in_ref[...])
    image_ref[...] = image
    old = old_ref[...]
    residual = scores_ref[...] - state_ref[2:3, :] * old
    scalars = [lane_sum(image * residual), lane_sum(image * image), lane_sum(image * old)]
    send_backward(image_ref, row_ref, split_ref, live_ref[0], scalars, out_ref, picked)


def third_gradient_kernel(
    live_ref, in_ref, split_ref, first_ref, second_ref, product_ref, state_ref,
    out_ref, keep_ref, later_ref,
):
    total = added(in_ref)
    old_norm, old_image_norm, old_step = state_ref[0:1, :], state_ref[1:2, :], state_ref[2:3, :]
    norm, straight, cross = scalars_of(total[WANT : WANT + 1], 3)
    ratio = norm / old_norm
    image_norm = straight + 2.0 * ratio * cross + ratio * ratio * old_image_norm
    step = norm / image_norm
    first, second = first_ref[...], second_ref[...]
    product = total[:WANT] + ratio * product_ref[...]
    third = second - step * product
    direction = second + ratio * first
    weights = old_step * first + step * direction
    keep_ref[0] = third[CAP:]
    keep_ref[1] = direction[CAP:]
    keep_ref[2] = weights[CAP:]
    later_ref[...] = stack_rows([norm, image_norm, step, ratio])
    send_forward(third[:CAP], split_ref, live_ref[0], jnp.zeros((1, TB), F32), out_ref)


def third_image_kernel(
    in_ref, hits_ref, scores_ref, first_ref, second_ref, state_ref, later_ref,
    out_ref, keep_ref,
):
    image = picked_sum(hits_ref[...], in_ref[...])
    first = first_ref[...]
    old = second_ref[...] + later_ref[3:4, :] * first
    residual = scores_ref[...] - state_ref[2:3, :] * first - later_ref[2:3, :] * old
    keep_ref[0] = image
    keep_ref[1] = old
    keep_ref[2] = residual
    scalars = [lane_sum(image * residual), lane_sum(image * image), lane_sum(image * old)]
    out_ref[...] = jnp.broadcast_to(scalar_row(scalars), (ROWS, TB))


def last_kernel(in_ref, keep_ref, image_ref, later_ref, weights_ref, residual_ref):
    norm, straight, cross = scalars_of(lane_sum(in_ref[...]), 3)
    ratio = norm / later_ref[0:1, :]
    image_norm = straight + 2.0 * ratio * cross + ratio * ratio * later_ref[1:2, :]
    step = norm / image_norm
    weights_ref[...] = keep_ref[2] + step * (keep_ref[0] + ratio * keep_ref[1])
    residual_ref[...] = image_ref[2] - step * (image_ref[0] + ratio * image_ref[1])


def call(kernel, outs, args, scratch=(), memory=None, room=16 * 2**20):
    def spec(x):
        scalar = x.dtype == jnp.int32
        return pl.BlockSpec(memory_space=memory or (pltpu.SMEM if scalar else pltpu.VMEM))

    return pl.pallas_call(
        kernel,
        out_shape=[jax.ShapeDtypeStruct(s, d) for s, d in outs],
        in_specs=[spec(a) for a in args],
        out_specs=[pl.BlockSpec(memory_space=pltpu.VMEM) for _ in outs],
        scratch_shapes=list(scratch),
        compiler_params=pltpu.CompilerParams(vmem_limit_bytes=room),
        name=kernel.__name__,
    )(*args)


def swap(x, axes, count):
    shape = x.shape
    if len(shape) == 2:
        x = x.reshape(count, shape[0] // count, 1, TB)
    return lax.all_to_all(x, axes, 0, 0, tiled=True).reshape(shape)


def local(tiles, tile_row, tile_col, tile_counts, scores):
    f = lambda *shape: (shape, F32)
    b = lambda *shape: (shape, BF16)
    near, cols = ("pair", "y"), ("x", "core")
    to_far, to_near = f(LINE, TB), f(NEAR, HAND, TB)
    to_cols = f(SIDE, TB)
    image_shape, state_shape = f(ROW_BLOCKS, TB), f(EXTRA, TB)
    picked = [pltpu.VMEM((CAP, TB), F32)]

    message, split = call(
        first_kernel,
        [to_far, b(CAP, 2 * TB, TB)],
        [tile_row, tile_col, tile_counts, tiles, scores],
        [
            pltpu.SMEM((CAP,), jnp.int32),
            pltpu.SMEM((CAP,), jnp.int32),
            pltpu.SMEM((1,), jnp.int32),
            pltpu.VMEM((CAP, TB, TB), F32),
            pltpu.VMEM((ROW_BLOCKS, TB), F32),
            *picked,
            pltpu.SemaphoreType.DMA((4 + PARTS,)),
        ],
        pltpu.HBM,
        62 * 2**20,
    )
    (message,) = call(relay_kernel, [f(NEAR, LINE + EXTRA, TB)], [swap(message, "far", FAR)])
    message, first, hand_hits = call(
        gathered_kernel,
        [to_cols, f(WANT, TB), b(NEAR * WANT, LINE)],
        [tile_row, tile_counts, swap(message, near, NEAR), split],
    )
    message, image, row_hits = call(
        first_image_kernel,
        [to_far, image_shape, b(ROW_BLOCKS, SIDE)],
        [tile_row, tile_counts, swap(message, cols, COLS), split, scores],
        picked,
    )
    (message,) = call(hand_kernel, [to_near], [swap(message, "far", FAR), hand_hits])
    message, product, second, state = call(
        second_gradient_kernel,
        [to_cols, f(WANT, TB), f(WANT, TB), state_shape],
        [tile_counts, swap(message, near, NEAR), split, first],
    )
    message, second_image = call(
        second_image_kernel,
        [to_far, image_shape],
        [tile_row, tile_counts, swap(message, cols, COLS), split, row_hits, scores, image, state],
        picked,
    )
    (message,) = call(hand_kernel, [to_near], [swap(message, "far", FAR), hand_hits])
    message, keep, later = call(
        third_gradient_kernel,
        [to_cols, f(3, SHARE, TB), state_shape],
        [tile_counts, swap(message, near, NEAR), split, first, second, product, state],
    )
    message, images = call(
        third_image_kernel,
        [f(ROWS, TB), f(3, ROW_BLOCKS, TB)],
        [swap(message, cols, COLS), row_hits, scores, image, second_image, state, later],
    )
    weights, residual = call(
        last_kernel,
        [f(SHARE, TB), image_shape],
        [swap(message, ("far", *near), ROWS), keep, images, later],
    )
    return weights, residual


def solution(mesh):
    rows, cols = ("far", "pair", "y"), ("x", "core")
    every = rows + cols
    fine = Mesh(mesh.devices.reshape(FAR, PAIR, Y, X, CORE), every)
    return jax.shard_map(
        local,
        mesh=fine,
        in_specs=(P(every, None, None), P(every), P(every), P(every), P(rows, None)),
        out_specs=(P(cols + rows, None), P(rows, None)),
        check_vma=False,
    )
```

```python
import functools

import jax
import jax.numpy as jnp
from jax import lax
from jax.experimental import pallas as pl
from jax.experimental.pallas import tpu as pltpu
from jax.sharding import Mesh, PartitionSpec as P


FAR, PAIR, Y, X, CORE = 8, 2, 4, 4, 2
NEAR = PAIR * Y
COLS = X * CORE
ROWS = FAR * NEAR
CAP = 24
TB = 128
ROW_BLOCKS = 256
SHARE = 16
WANT = CAP + SHARE
EXTRA = 8
MSG = CAP + 1
LINE = FAR * MSG
SIDE = COLS * MSG
HAND = WANT + EXTRA
PARTS = 3
INFO = 2 * CAP + EXTRA
F32 = jnp.float32
BF16 = jnp.bfloat16


def iota(shape, dim):
    return lax.broadcasted_iota(jnp.int32, shape, dim)


def two_parts(x):
    high = x.astype(BF16).astype(F32)
    return high, x - high


def side_by_side(x):
    high, low = two_parts(x)
    return jnp.concatenate([high, low], axis=1).astype(BF16)


def picked_sum(hits, values):
    out = jnp.dot(hits, side_by_side(values), preferred_element_type=F32)
    return out[:, :TB] + out[:, TB:]


def times_tiles(vectors, split_ref, live, transposed):
    sub = iota((8, TB), 0)
    groups = []
    for g in range(CAP // 8):
        high, low = two_parts(vectors[8 * g : 8 * g + 8])
        both = jnp.concatenate([high, low], axis=0).astype(BF16)
        if transposed:
            both = jnp.concatenate([both, both], axis=1)
        total = jnp.zeros((8, TB), F32)
        for k in range(8):
            tile = split_ref[8 * g + k]
            if transposed:
                out = jnp.dot(both, tile, preferred_element_type=F32)
            else:
                out = lax.dot_general(
                    both, tile, (((1,), (1,)), ((), ())), preferred_element_type=F32
                )
                out = out[:, :TB] + out[:, TB:]
            total = jnp.where(sub == k, out[:8] + out[8:], total)
        groups.append(jnp.where(live[8 * g : 8 * g + 8] > 0.0, total, 0.0))
    return jnp.concatenate(groups, axis=0)


def split_tiles(tiles, split_ref, start, stop):
    for j in range(start, stop):
        high, low = two_parts(tiles[j])
        split_ref[j, :TB, :] = high.astype(BF16)
        split_ref[j, TB:, :] = low.astype(BF16)


def pick_rows(source, row_ref, picked):
    for j in range(CAP):
        picked[j : j + 1, :] = source[pl.ds(row_ref[j], 1), :]


def hits_of(wanted, lane_rows, width):
    pieces = [jnp.where(wanted == row, 1.0, 0.0) for row in lane_rows]
    return jnp.concatenate(pieces, axis=1)[:, :width].astype(BF16)


def index_row(index_ref, live, base):
    lane = iota((1, TB), 1)
    row = jnp.zeros((1, TB), F32)
    for j in range(CAP):
        value = jnp.where(j < live, index_ref[j] + 1, 0).astype(F32)
        row = jnp.where(lane == lax.rem(base + j, TB), value, row)
    return row


def index_lanes(in_ref, count):
    lane = iota((1, TB), 1)
    rows = []
    for k in range(-(-count * MSG // TB)):
        row = jnp.zeros((1, TB), F32)
        for i in range(count):
            low, high = MSG * i - TB * k, MSG * i + CAP - TB * k
            if high > 0 and low < TB:
                mine = (lane >= low) & (lane < high)
                row = jnp.where(mine, in_ref[MSG * i + CAP : MSG * (i + 1), :], row)
        rows.append(row)
    return rows


def send_to_all(out_ref, count, sums, row):
    message = jnp.concatenate([sums, row], axis=0)
    for i in range(count):
        out_ref[MSG * i : MSG * (i + 1), :] = message


def extra_sum(in_ref, count):
    row = in_ref[CAP : CAP + 1, :]
    for i in range(1, count):
        row = row + in_ref[MSG * i + CAP : MSG * (i + 1), :]
    return row


def scalar_row(rows):
    sums = jnp.sum(stack_rows(rows), axis=1, keepdims=True)
    apart = jnp.where(iota((EXTRA, TB), 0) == iota((EXTRA, TB), 1), sums, 0.0)
    return jnp.sum(apart, axis=0, keepdims=True)


def scalars_of(row, count):
    apart = jnp.where(iota((EXTRA, TB), 0) == iota((EXTRA, TB), 1), row, 0.0)
    sums = jnp.sum(apart, axis=1, keepdims=True)
    return [sums[k : k + 1] for k in range(count)]


def lane_sum(x):
    return jnp.sum(x, axis=0, keepdims=True)


def stack_rows(rows):
    sub = iota((EXTRA, TB), 0)
    out = jnp.zeros((EXTRA, TB), F32)
    for k, row in enumerate(rows):
        out = jnp.where(sub == k, row, out)
    return out


def first_kernel(
    row_hbm, col_hbm, live_hbm, tiles_hbm, scores_hbm, out_ref, info_ref,
    row_ref, col_ref, live_ref, tiles, scores, split_ref, picked, done,
):
    part = CAP // PARTS
    copies = [
        pltpu.make_async_copy(row_hbm, row_ref, done.at[0]),
        pltpu.make_async_copy(col_hbm, col_ref, done.at[1]),
        pltpu.make_async_copy(live_hbm, live_ref, done.at[2]),
        pltpu.make_async_copy(scores_hbm, scores, done.at[3]),
    ]
    for i in range(PARTS):
        some = pl.ds(part * i, part)
        copies.append(pltpu.make_async_copy(tiles_hbm.at[some], tiles.at[some], done.at[4 + i]))
    for copy in copies:
        copy.start()
    for copy in copies[:4]:
        copy.wait()
    live = live_ref[0]
    pick_rows(scores, row_ref, picked)
    row = index_row(col_ref, live, lax.axis_index("far") * MSG)
    sub = iota((CAP, TB), 0)
    mask = jnp.where(sub < live, 1.0, 0.0)
    own = jnp.full((CAP, TB), -1.0, F32)
    for j in range(CAP):
        own = jnp.where(sub == j, jnp.where(j < live, row_ref[j] + 1, -1).astype(F32), own)
    place = lax.axis_index("x") * CORE + lax.axis_index("core")
    info_ref[:CAP, :] = mask
    info_ref[CAP : 2 * CAP, :] = own
    info_ref[2 * CAP :, :] = stack_rows([index_row(row_ref, live, place * MSG)])
    for i in range(PARTS):
        copies[4 + i].wait()
        split_tiles(tiles, split_ref, part * i, part * (i + 1))
    sums = times_tiles(picked[...], split_ref, mask, True)
    send_to_all(out_ref, FAR, sums, row)


def relay_kernel(in_ref, out_ref):
    rows = index_lanes(in_ref, FAR)
    for i in range(NEAR):
        out_ref[i, :LINE, :] = in_ref[...]
        out_ref[i, LINE:, :] = stack_rows(rows)


def send_forward(vectors, split_ref, info_ref, row, out_ref):
    send_to_all(out_ref, COLS, times_tiles(vectors, split_ref, info_ref[:CAP, :], False), row)


def gathered_kernel(
    info_ref, in_ref, tiles_ref, out_ref, gradient_ref, hits_ref, split_ref
):
    split_tiles(tiles_ref, split_ref, 0, CAP)
    far = lax.axis_index("far")
    near = lax.axis_index("pair") * Y + lax.axis_index("y")
    lines = -(-LINE // TB)
    index = [[in_ref[i, LINE + k : LINE + k + 1, :] for k in range(lines)] for i in range(NEAR)]
    own_rows = index[0]
    for i in range(1, NEAR):
        own_rows = [jnp.where(near == i, new, old) for new, old in zip(index[i], own_rows)]
    own_wanted = jnp.zeros((WANT, 1), F32)
    lane, sub = iota((CAP, TB), 1), iota((CAP, TB), 0)
    for i in range(NEAR):
        found = jnp.zeros((CAP, TB), F32)
        for k in range(lines):
            found = jnp.where(lane + k * TB == sub + far * MSG, index[i][k], found)
        tile_part = jnp.sum(found, axis=1, keepdims=True)
        tile_part = jnp.where(tile_part == 0.0, -1.0, tile_part)
        share_part = ((far * NEAR + i) * SHARE + 1 + iota((SHARE, 1), 0)).astype(F32)
        wanted = jnp.concatenate([tile_part, share_part], axis=0)
        hits_ref[WANT * i : WANT * (i + 1), :] = hits_of(wanted, own_rows, LINE)
        own_wanted = jnp.where(near == i, wanted, own_wanted)
    gradient = jnp.zeros((WANT, TB), F32)
    for i in range(NEAR):
        gradient += picked_sum(hits_of(own_wanted, index[i], LINE), in_ref[i, :LINE, :])
    gradient_ref[...] = gradient
    send_forward(gradient[:CAP], split_ref, info_ref, info_ref[2 * CAP : 2 * CAP + 1, :], out_ref)


def send_backward(picked, split_ref, info_ref, scalars, out_ref):
    sums = times_tiles(picked, split_ref, info_ref[:CAP, :], True)
    send_to_all(out_ref, FAR, sums, scalar_row(scalars))


def first_image_kernel(
    info_ref, in_ref, split_ref, scores_ref, out_ref, image_ref, hits_ref
):
    wanted = (iota((ROW_BLOCKS, 1), 0) + 1).astype(F32)
    wanted = jnp.concatenate([wanted, info_ref[CAP : 2 * CAP, :1]], axis=0)
    hits = hits_of(wanted, index_lanes(in_ref, COLS), SIDE)
    hits_ref[...] = hits
    sums = picked_sum(hits, in_ref[...])
    image = sums[:ROW_BLOCKS]
    image_ref[...] = image
    scalars = [lane_sum(image * scores_ref[...]), lane_sum(image * image)]
    send_backward(sums[ROW_BLOCKS:], split_ref, info_ref, scalars, out_ref)


def hand_kernel(in_ref, hits_ref, out_ref):
    extra = jnp.broadcast_to(extra_sum(in_ref, FAR), (EXTRA, TB))
    sums = picked_sum(hits_ref[...], in_ref[...])
    for i in range(NEAR):
        out_ref[i, :WANT, :] = sums[WANT * i : WANT * (i + 1)]
        out_ref[i, WANT:, :] = extra


def added(in_ref):
    total = in_ref[0]
    for i in range(1, in_ref.shape[0]):
        total = total + in_ref[i]
    return total


def second_gradient_kernel(
    info_ref, in_ref, split_ref, gradient_ref, out_ref, product_ref, next_ref, state_ref
):
    total = added(in_ref)
    product = total[:WANT]
    norm, image_norm = scalars_of(total[WANT : WANT + 1], 2)
    step = norm / image_norm
    following = gradient_ref[...] - step * product
    product_ref[...] = product
    next_ref[...] = following
    state_ref[...] = stack_rows([norm, image_norm, step])
    send_forward(following[:CAP], split_ref, info_ref, jnp.zeros((1, TB), F32), out_ref)


def second_image_kernel(
    info_ref, in_ref, split_ref, hits_ref, scores_ref, old_ref, state_ref, out_ref, image_ref
):
    sums = picked_sum(hits_ref[...], in_ref[...])
    image = sums[:ROW_BLOCKS]
    image_ref[...] = image
    old = old_ref[...]
    residual = scores_ref[...] - state_ref[2:3, :] * old
    scalars = [lane_sum(image * residual), lane_sum(image * image), lane_sum(image * old)]
    send_backward(sums[ROW_BLOCKS:], split_ref, info_ref, scalars, out_ref)


def third_gradient_kernel(
    info_ref, in_ref, split_ref, first_ref, second_ref, product_ref, state_ref,
    out_ref, keep_ref, later_ref,
):
    total = added(in_ref)
    old_norm, old_image_norm, old_step = state_ref[0:1, :], state_ref[1:2, :], state_ref[2:3, :]
    norm, straight, cross = scalars_of(total[WANT : WANT + 1], 3)
    ratio = norm / old_norm
    image_norm = straight + 2.0 * ratio * cross + ratio * ratio * old_image_norm
    step = norm / image_norm
    first, second = first_ref[...], second_ref[...]
    product = total[:WANT] + ratio * product_ref[...]
    third = second - step * product
    direction = second + ratio * first
    weights = old_step * first + step * direction
    keep_ref[0] = third[CAP:]
    keep_ref[1] = direction[CAP:]
    keep_ref[2] = weights[CAP:]
    later_ref[...] = stack_rows([norm, image_norm, step, ratio])
    send_forward(third[:CAP], split_ref, info_ref, jnp.zeros((1, TB), F32), out_ref)


def third_image_kernel(
    in_ref, hits_ref, scores_ref, first_ref, second_ref, state_ref, later_ref,
    out_ref, keep_ref,
):
    image = picked_sum(hits_ref[:ROW_BLOCKS, :], in_ref[...])
    first = first_ref[...]
    old = second_ref[...] + later_ref[3:4, :] * first
    residual = scores_ref[...] - state_ref[2:3, :] * first - later_ref[2:3, :] * old
    keep_ref[0] = image
    keep_ref[1] = old
    keep_ref[2] = residual
    scalars = [lane_sum(image * residual), lane_sum(image * image), lane_sum(image * old)]
    out_ref[...] = jnp.broadcast_to(scalar_row(scalars), (ROWS, TB))


def last_kernel(in_ref, keep_ref, image_ref, later_ref, weights_ref, residual_ref):
    norm, straight, cross = scalars_of(lane_sum(in_ref[...]), 3)
    ratio = norm / later_ref[0:1, :]
    image_norm = straight + 2.0 * ratio * cross + ratio * ratio * later_ref[1:2, :]
    step = norm / image_norm
    weights_ref[...] = keep_ref[2] + step * (keep_ref[0] + ratio * keep_ref[1])
    residual_ref[...] = image_ref[2] - step * (image_ref[0] + ratio * image_ref[1])


def call(kernel, outs, args, scratch=(), memory=None, room=16 * 2**20):
    def spec(x):
        scalar = x.dtype == jnp.int32
        return pl.BlockSpec(memory_space=memory or (pltpu.SMEM if scalar else pltpu.VMEM))

    return pl.pallas_call(
        kernel,
        out_shape=[jax.ShapeDtypeStruct(s, d) for s, d in outs],
        in_specs=[spec(a) for a in args],
        out_specs=[pl.BlockSpec(memory_space=pltpu.VMEM) for _ in outs],
        scratch_shapes=list(scratch),
        compiler_params=pltpu.CompilerParams(vmem_limit_bytes=room),
        name=kernel.__name__,
    )(*args)


def swap(x, axes, count):
    shape = x.shape
    if len(shape) == 2:
        x = x.reshape(count, shape[0] // count, 1, TB)
    return lax.all_to_all(x, axes, 0, 0, tiled=True).reshape(shape)


def local(tiles, tile_row, tile_col, tile_counts, scores):
    f = lambda *shape: (shape, F32)
    b = lambda *shape: (shape, BF16)
    near, cols = ("pair", "y"), ("x", "core")
    to_far, to_near = f(LINE, TB), f(NEAR, HAND, TB)
    to_cols = f(SIDE, TB)
    image_shape, state_shape = f(ROW_BLOCKS, TB), f(EXTRA, TB)

    message, info = call(
        first_kernel,
        [to_far, f(INFO, TB)],
        [tile_row, tile_col, tile_counts, tiles, scores],
        [
            pltpu.SMEM((CAP,), jnp.int32),
            pltpu.SMEM((CAP,), jnp.int32),
            pltpu.SMEM((1,), jnp.int32),
            pltpu.VMEM((CAP, TB, TB), F32),
            pltpu.VMEM((ROW_BLOCKS, TB), F32),
            pltpu.VMEM((CAP, 2 * TB, TB), BF16),
            pltpu.VMEM((CAP, TB), F32),
            pltpu.SemaphoreType.DMA((4 + PARTS,)),
        ],
        pltpu.HBM,
        62 * 2**20,
    )
    (message,) = call(relay_kernel, [f(NEAR, LINE + EXTRA, TB)], [swap(message, "far", FAR)])
    message, first, hand_hits, split = call(
        gathered_kernel,
        [to_cols, f(WANT, TB), b(NEAR * WANT, LINE), b(CAP, 2 * TB, TB)],
        [info, swap(message, near, NEAR), tiles],
    )
    message, image, row_hits = call(
        first_image_kernel,
        [to_far, image_shape, b(ROW_BLOCKS + CAP, SIDE)],
        [info, swap(message, cols, COLS), split, scores],
    )
    (message,) = call(hand_kernel, [to_near], [swap(message, "far", FAR), hand_hits])
    message, product, second, state = call(
        second_gradient_kernel,
        [to_cols, f(WANT, TB), f(WANT, TB), state_shape],
        [info, swap(message, near, NEAR), split, first],
    )
    message, second_image = call(
        second_image_kernel,
        [to_far, image_shape],
        [info, swap(message, cols, COLS), split, row_hits, scores, image, state],
    )
    (message,) = call(hand_kernel, [to_near], [swap(message, "far", FAR), hand_hits])
    message, keep, later = call(
        third_gradient_kernel,
        [to_cols, f(3, SHARE, TB), state_shape],
        [info, swap(message, near, NEAR), split, first, second, product, state],
    )
    message, images = call(
        third_image_kernel,
        [f(ROWS, TB), f(3, ROW_BLOCKS, TB)],
        [swap(message, cols, COLS), row_hits, scores, image, second_image, state, later],
    )
    weights, residual = call(
        last_kernel,
        [f(SHARE, TB), image_shape],
        [swap(message, ("far", *near), ROWS), keep, images, later],
    )
    return weights, residual


def solution(mesh):
    rows, cols = ("far", "pair", "y"), ("x", "core")
    every = rows + cols
    fine = Mesh(mesh.devices.reshape(FAR, PAIR, Y, X, CORE), every)
    return jax.shard_map(
        local,
        mesh=fine,
        in_specs=(P(every, None, None), P(every), P(every), P(every), P(rows, None)),
        out_specs=(P(cols + rows, None), P(rows, None)),
        check_vma=False,
    )
```

```python
import functools

import jax
import jax.numpy as jnp
from jax import lax
from jax.experimental import pallas as pl
from jax.experimental.pallas import tpu as pltpu
from jax.sharding import PartitionSpec as P


FAR, NEAR, COLS = 8, 8, 8
ROWS = FAR * NEAR
LEAD = 4
CAP = 24
TB = 128
ROW_BLOCKS = 256
SHARE = 16
WANT = CAP + SHARE
EXTRA = 8
MSG = CAP + 1
LINE = FAR * MSG
SIDE = COLS * MSG
HAND = WANT + EXTRA
PARTS = 3
INFO = 2 * CAP + EXTRA
F32 = jnp.float32
BF16 = jnp.bfloat16


def places():
    row = lax.axis_index("rows")
    return lax.div(row, NEAR), lax.rem(row, NEAR)


def iota(shape, dim):
    return lax.broadcasted_iota(jnp.int32, shape, dim)


def two_parts(x):
    high = x.astype(BF16).astype(F32)
    return high, x - high


def side_by_side(x):
    high, low = two_parts(x)
    return jnp.concatenate([high, low], axis=1).astype(BF16)


def picked_sum(hits, values):
    out = jnp.dot(hits, side_by_side(values), preferred_element_type=F32)
    return out[:, :TB] + out[:, TB:]


def times_tiles(vectors, split_ref, live, transposed):
    sub = iota((8, TB), 0)
    groups = []
    for g in range(CAP // 8):
        high, low = two_parts(vectors[8 * g : 8 * g + 8])
        both = jnp.concatenate([high, low], axis=0).astype(BF16)
        if transposed:
            both = jnp.concatenate([both, both], axis=1)
        total = jnp.zeros((8, TB), F32)
        for k in range(8):
            tile = split_ref[8 * g + k]
            if transposed:
                out = jnp.dot(both, tile, preferred_element_type=F32)
            else:
                out = lax.dot_general(
                    both, tile, (((1,), (1,)), ((), ())), preferred_element_type=F32
                )
                out = out[:, :TB] + out[:, TB:]
            total = jnp.where(sub == k, out[:8] + out[8:], total)
        groups.append(jnp.where(live[8 * g : 8 * g + 8] > 0.0, total, 0.0))
    return jnp.concatenate(groups, axis=0)


def split_tiles(tiles, split_ref, start, stop):
    for j in range(start, stop):
        high, low = two_parts(tiles[j])
        split_ref[j, :TB, :] = high.astype(BF16)
        split_ref[j, TB:, :] = low.astype(BF16)


def pick_rows(source, row_ref, picked):
    for j in range(CAP):
        picked[j : j + 1, :] = source[pl.ds(row_ref[j], 1), :]


def hits_of(wanted, lane_rows, width):
    pieces = [jnp.where(wanted == row, 1.0, 0.0) for row in lane_rows]
    return jnp.concatenate(pieces, axis=1)[:, :width].astype(BF16)


def index_row(index_ref, live, base):
    lane = iota((1, TB), 1)
    row = jnp.zeros((1, TB), F32)
    for j in range(CAP):
        value = jnp.where(j < live, index_ref[j] + 1, 0).astype(F32)
        row = jnp.where(lane == lax.rem(base + j, TB), value, row)
    return row


def index_lanes(in_ref, count):
    lane = iota((1, TB), 1)
    rows = []
    for k in range(-(-count * MSG // TB)):
        row = jnp.zeros((1, TB), F32)
        for i in range(count):
            low, high = MSG * i - TB * k, MSG * i + CAP - TB * k
            if high > 0 and low < TB:
                mine = (lane >= low) & (lane < high)
                row = jnp.where(mine, in_ref[MSG * i + CAP : MSG * (i + 1), :], row)
        rows.append(row)
    return rows


def send_to_all(out_ref, count, sums, row):
    message = jnp.concatenate([sums, row], axis=0)
    for i in range(count):
        out_ref[MSG * i : MSG * (i + 1), :] = message


def extra_sum(in_ref, count):
    row = in_ref[CAP : CAP + 1, :]
    for i in range(1, count):
        row = row + in_ref[MSG * i + CAP : MSG * (i + 1), :]
    return row


def scalar_row(rows):
    sums = jnp.sum(stack_rows(rows), axis=1, keepdims=True)
    apart = jnp.where(iota((EXTRA, TB), 0) == iota((EXTRA, TB), 1), sums, 0.0)
    return jnp.sum(apart, axis=0, keepdims=True)


def scalars_of(row, count):
    apart = jnp.where(iota((EXTRA, TB), 0) == iota((EXTRA, TB), 1), row, 0.0)
    sums = jnp.sum(apart, axis=1, keepdims=True)
    return [sums[k : k + 1] for k in range(count)]


def lane_sum(x):
    return jnp.sum(x, axis=0, keepdims=True)


def stack_rows(rows):
    sub = iota((EXTRA, TB), 0)
    out = jnp.zeros((EXTRA, TB), F32)
    for k, row in enumerate(rows):
        out = jnp.where(sub == k, row, out)
    return out


def first_kernel(
    row_hbm, col_hbm, live_hbm, tiles_hbm, scores_hbm, out_ref, info_ref,
    row_ref, col_ref, live_ref, tiles, scores, split_ref, picked, done,
):
    part = CAP // PARTS
    copies = [
        pltpu.make_async_copy(row_hbm, row_ref, done.at[0]),
        pltpu.make_async_copy(col_hbm, col_ref, done.at[1]),
        pltpu.make_async_copy(live_hbm, live_ref, done.at[2]),
        pltpu.make_async_copy(scores_hbm, scores, done.at[3]),
    ]
    for i in range(PARTS):
        some = pl.ds(part * i, part)
        copies.append(pltpu.make_async_copy(tiles_hbm.at[some], tiles.at[some], done.at[4 + i]))
    for copy in copies:
        copy.start()
    for copy in copies[:4]:
        copy.wait()
    live = live_ref[0]
    pick_rows(scores, row_ref, picked)
    far, _ = places()
    row = index_row(col_ref, live, lax.rem(far + FAR - LEAD, FAR) * MSG)
    sub = iota((CAP, TB), 0)
    mask = jnp.where(sub < live, 1.0, 0.0)
    own = jnp.full((CAP, TB), -1.0, F32)
    for j in range(CAP):
        own = jnp.where(sub == j, jnp.where(j < live, row_ref[j] + 1, -1).astype(F32), own)
    place = lax.axis_index("cols")
    info_ref[:CAP, :] = mask
    info_ref[CAP : 2 * CAP, :] = own
    info_ref[2 * CAP :, :] = stack_rows([index_row(row_ref, live, place * MSG)])
    for i in range(PARTS):
        copies[4 + i].wait()
        split_tiles(tiles, split_ref, part * i, part * (i + 1))
    sums = times_tiles(picked[...], split_ref, mask, True)
    send_to_all(out_ref, FAR, sums, row)


def relay_kernel(in_ref, out_ref):
    rows = index_lanes(in_ref, FAR)
    for i in range(NEAR):
        out_ref[i, :LINE, :] = in_ref[...]
        out_ref[i, LINE:, :] = stack_rows(rows)


def send_forward(vectors, split_ref, info_ref, row, out_ref):
    send_to_all(out_ref, COLS, times_tiles(vectors, split_ref, info_ref[:CAP, :], False), row)


def gathered_kernel(
    info_ref, in_ref, tiles_ref, out_ref, gradient_ref, hits_ref, split_ref
):
    split_tiles(tiles_ref, split_ref, 0, CAP)
    far, near = places()
    slot = lax.rem(far + FAR - LEAD, FAR)
    lines = -(-LINE // TB)
    index = [[in_ref[i, LINE + k : LINE + k + 1, :] for k in range(lines)] for i in range(NEAR)]
    own_rows = index[0]
    for i in range(1, NEAR):
        own_rows = [jnp.where(near == i, new, old) for new, old in zip(index[i], own_rows)]
    own_wanted = jnp.zeros((WANT, 1), F32)
    lane, sub = iota((CAP, TB), 1), iota((CAP, TB), 0)
    for i in range(NEAR):
        found = jnp.zeros((CAP, TB), F32)
        for k in range(lines):
            found = jnp.where(lane + k * TB == sub + slot * MSG, index[i][k], found)
        tile_part = jnp.sum(found, axis=1, keepdims=True)
        tile_part = jnp.where(tile_part == 0.0, -1.0, tile_part)
        share_part = ((far * NEAR + i) * SHARE + 1 + iota((SHARE, 1), 0)).astype(F32)
        wanted = jnp.concatenate([tile_part, share_part], axis=0)
        hits_ref[WANT * i : WANT * (i + 1), :] = hits_of(wanted, own_rows, LINE)
        own_wanted = jnp.where(near == i, wanted, own_wanted)
    gradient = jnp.zeros((WANT, TB), F32)
    for i in range(NEAR):
        gradient += picked_sum(hits_of(own_wanted, index[i], LINE), in_ref[i, :LINE, :])
    gradient_ref[...] = gradient
    send_forward(gradient[:CAP], split_ref, info_ref, info_ref[2 * CAP : 2 * CAP + 1, :], out_ref)


def send_backward(picked, split_ref, info_ref, scalars, out_ref):
    sums = times_tiles(picked, split_ref, info_ref[:CAP, :], True)
    send_to_all(out_ref, FAR, sums, scalar_row(scalars))


def first_image_kernel(
    info_ref, in_ref, split_ref, scores_ref, out_ref, image_ref, hits_ref
):
    wanted = (iota((ROW_BLOCKS, 1), 0) + 1).astype(F32)
    wanted = jnp.concatenate([wanted, info_ref[CAP : 2 * CAP, :1]], axis=0)
    hits = hits_of(wanted, index_lanes(in_ref, COLS), SIDE)
    hits_ref[...] = hits
    sums = picked_sum(hits, in_ref[...])
    image = sums[:ROW_BLOCKS]
    image_ref[...] = image
    scalars = [lane_sum(image * scores_ref[...]), lane_sum(image * image)]
    send_backward(sums[ROW_BLOCKS:], split_ref, info_ref, scalars, out_ref)


def hand_kernel(in_ref, hits_ref, out_ref):
    extra = jnp.broadcast_to(extra_sum(in_ref, FAR), (EXTRA, TB))
    sums = picked_sum(hits_ref[...], in_ref[...])
    for i in range(NEAR):
        out_ref[i, :WANT, :] = sums[WANT * i : WANT * (i + 1)]
        out_ref[i, WANT:, :] = extra


def added(in_ref):
    total = in_ref[0]
    for i in range(1, in_ref.shape[0]):
        total = total + in_ref[i]
    return total


def second_gradient_kernel(
    info_ref, in_ref, split_ref, gradient_ref, out_ref, product_ref, next_ref, state_ref
):
    total = added(in_ref)
    product = total[:WANT]
    norm, image_norm = scalars_of(total[WANT : WANT + 1], 2)
    step = norm / image_norm
    following = gradient_ref[...] - step * product
    product_ref[...] = product
    next_ref[...] = following
    state_ref[...] = stack_rows([norm, image_norm, step])
    send_forward(following[:CAP], split_ref, info_ref, jnp.zeros((1, TB), F32), out_ref)


def second_image_kernel(
    info_ref, in_ref, split_ref, hits_ref, scores_ref, old_ref, state_ref, out_ref, image_ref
):
    sums = picked_sum(hits_ref[...], in_ref[...])
    image = sums[:ROW_BLOCKS]
    image_ref[...] = image
    old = old_ref[...]
    residual = scores_ref[...] - state_ref[2:3, :] * old
    scalars = [lane_sum(image * residual), lane_sum(image * image), lane_sum(image * old)]
    send_backward(sums[ROW_BLOCKS:], split_ref, info_ref, scalars, out_ref)


def third_gradient_kernel(
    info_ref, in_ref, split_ref, first_ref, second_ref, product_ref, state_ref,
    out_ref, keep_ref, later_ref,
):
    total = added(in_ref)
    old_norm, old_image_norm, old_step = state_ref[0:1, :], state_ref[1:2, :], state_ref[2:3, :]
    norm, straight, cross = scalars_of(total[WANT : WANT + 1], 3)
    ratio = norm / old_norm
    image_norm = straight + 2.0 * ratio * cross + ratio * ratio * old_image_norm
    step = norm / image_norm
    first, second = first_ref[...], second_ref[...]
    product = total[:WANT] + ratio * product_ref[...]
    third = second - step * product
    direction = second + ratio * first
    weights = old_step * first + step * direction
    keep_ref[0] = third[CAP:]
    keep_ref[1] = direction[CAP:]
    keep_ref[2] = weights[CAP:]
    later_ref[...] = stack_rows([norm, image_norm, step, ratio])
    send_forward(third[:CAP], split_ref, info_ref, jnp.zeros((1, TB), F32), out_ref)


def third_image_kernel(
    in_ref, hits_ref, scores_ref, first_ref, second_ref, state_ref, later_ref,
    out_ref, keep_ref,
):
    image = picked_sum(hits_ref[:ROW_BLOCKS, :], in_ref[...])
    first = first_ref[...]
    old = second_ref[...] + later_ref[3:4, :] * first
    residual = scores_ref[...] - state_ref[2:3, :] * first - later_ref[2:3, :] * old
    keep_ref[0] = image
    keep_ref[1] = old
    keep_ref[2] = residual
    scalars = [lane_sum(image * residual), lane_sum(image * image), lane_sum(image * old)]
    out_ref[...] = jnp.broadcast_to(scalar_row(scalars), (ROWS, TB))


def last_kernel(in_ref, keep_ref, image_ref, later_ref, weights_ref, residual_ref):
    norm, straight, cross = scalars_of(lane_sum(in_ref[...]), 3)
    ratio = norm / later_ref[0:1, :]
    image_norm = straight + 2.0 * ratio * cross + ratio * ratio * later_ref[1:2, :]
    step = norm / image_norm
    weights_ref[...] = keep_ref[2] + step * (keep_ref[0] + ratio * keep_ref[1])
    residual_ref[...] = image_ref[2] - step * (image_ref[0] + ratio * image_ref[1])


def call(kernel, outs, args, scratch=(), memory=None, room=16 * 2**20):
    def spec(x):
        scalar = x.dtype == jnp.int32
        return pl.BlockSpec(memory_space=memory or (pltpu.SMEM if scalar else pltpu.VMEM))

    return pl.pallas_call(
        kernel,
        out_shape=[jax.ShapeDtypeStruct(s, d) for s, d in outs],
        in_specs=[spec(a) for a in args],
        out_specs=[pl.BlockSpec(memory_space=pltpu.VMEM) for _ in outs],
        scratch_shapes=list(scratch),
        compiler_params=pltpu.CompilerParams(vmem_limit_bytes=room),
        name=kernel.__name__,
    )(*args)


FAR_ORDER = [(LEAD + i) % FAR for i in range(FAR)]
GROUPS = {
    "far": [[far * NEAR + near for far in FAR_ORDER] for near in range(NEAR)],
    "near": [[far * NEAR + near for near in range(NEAR)] for far in range(FAR)],
    "rows": [[far * NEAR + near for far in FAR_ORDER for near in range(NEAR)]],
    "cols": None,
}


def swap(x, kind, count):
    shape = x.shape
    if len(shape) == 2:
        x = x.reshape(count, shape[0] // count, 1, TB)
    axis, groups = "cols" if kind == "cols" else "rows", GROUPS[kind]
    return lax.all_to_all(x, axis, 0, 0, axis_index_groups=groups, tiled=True).reshape(shape)


def local(tiles, tile_row, tile_col, tile_counts, scores):
    f = lambda *shape: (shape, F32)
    b = lambda *shape: (shape, BF16)
    to_far, to_near = f(LINE, TB), f(NEAR, HAND, TB)
    to_cols = f(SIDE, TB)
    image_shape, state_shape = f(ROW_BLOCKS, TB), f(EXTRA, TB)

    message, info = call(
        first_kernel,
        [to_far, f(INFO, TB)],
        [tile_row, tile_col, tile_counts, tiles, scores],
        [
            pltpu.SMEM((CAP,), jnp.int32),
            pltpu.SMEM((CAP,), jnp.int32),
            pltpu.SMEM((1,), jnp.int32),
            pltpu.VMEM((CAP, TB, TB), F32),
            pltpu.VMEM((ROW_BLOCKS, TB), F32),
            pltpu.VMEM((CAP, 2 * TB, TB), BF16),
            pltpu.VMEM((CAP, TB), F32),
            pltpu.SemaphoreType.DMA((4 + PARTS,)),
        ],
        pltpu.HBM,
        62 * 2**20,
    )
    (message,) = call(relay_kernel, [f(NEAR, LINE + EXTRA, TB)], [swap(message, "far", FAR)])
    message, first, hand_hits, split = call(
        gathered_kernel,
        [to_cols, f(WANT, TB), b(NEAR * WANT, LINE), b(CAP, 2 * TB, TB)],
        [info, swap(message, "near", NEAR), tiles],
    )
    message, image, row_hits = call(
        first_image_kernel,
        [to_far, image_shape, b(ROW_BLOCKS + CAP, SIDE)],
        [info, swap(message, "cols", COLS), split, scores],
    )
    (message,) = call(hand_kernel, [to_near], [swap(message, "far", FAR), hand_hits])
    message, product, second, state = call(
        second_gradient_kernel,
        [to_cols, f(WANT, TB), f(WANT, TB), state_shape],
        [info, swap(message, "near", NEAR), split, first],
    )
    message, second_image = call(
        second_image_kernel,
        [to_far, image_shape],
        [info, swap(message, "cols", COLS), split, row_hits, scores, image, state],
    )
    (message,) = call(hand_kernel, [to_near], [swap(message, "far", FAR), hand_hits])
    message, keep, later = call(
        third_gradient_kernel,
        [to_cols, f(3, SHARE, TB), state_shape],
        [info, swap(message, "near", NEAR), split, first, second, product, state],
    )
    message, images = call(
        third_image_kernel,
        [f(ROWS, TB), f(3, ROW_BLOCKS, TB)],
        [swap(message, "cols", COLS), row_hits, scores, image, second_image, state, later],
    )
    weights, residual = call(
        last_kernel,
        [f(SHARE, TB), image_shape],
        [swap(message, "rows", ROWS), keep, images, later],
    )
    return weights, residual


def solution(mesh):
    every = ("rows", "cols")
    return jax.shard_map(
        local,
        mesh=mesh,
        in_specs=(P(every, None, None), P(every), P(every), P(every), P("rows", None)),
        out_specs=(P(("cols", "rows"), None), P("rows", None)),
        check_vma=False,
    )
```

```python
import functools

import jax
import jax.numpy as jnp
from jax import lax
from jax.experimental import pallas as pl
from jax.experimental.pallas import tpu as pltpu
from jax.sharding import PartitionSpec as P


FAR, NEAR, COLS = 8, 8, 8
ROWS = FAR * NEAR
FAR_ORDER = [4, 0, 1, 7, 2, 6, 3, 5]
NEAR_ORDER = [2, 3, 4, 5, 6, 7, 0, 1]
COL_ORDER = [5, 1, 7, 3, 4, 0, 6, 2]
CAP = 24
TB = 128
ROW_BLOCKS = 256
SHARE = 16
WANT = CAP + SHARE
EXTRA = 8
MSG = CAP + 1
LINE = FAR * MSG
SIDE = COLS * MSG
HAND = WANT + EXTRA
PARTS = 3
INFO = 2 * CAP + EXTRA
F32 = jnp.float32
BF16 = jnp.bfloat16


def places():
    row = lax.axis_index("rows")
    return lax.div(row, NEAR), lax.rem(row, NEAR)


def slot_of(place, order):
    slot = 0
    for i, member in enumerate(order):
        slot = jnp.where(place == member, i, slot)
    return slot


def iota(shape, dim):
    return lax.broadcasted_iota(jnp.int32, shape, dim)


def two_parts(x):
    high = x.astype(BF16).astype(F32)
    return high, x - high


def side_by_side(x):
    high, low = two_parts(x)
    return jnp.concatenate([high, low], axis=1).astype(BF16)


def picked_sum(hits, values):
    out = jnp.dot(hits, side_by_side(values), preferred_element_type=F32)
    return out[:, :TB] + out[:, TB:]


def times_tiles(vectors, split_ref, live, transposed):
    sub = iota((8, TB), 0)
    groups = []
    for g in range(CAP // 8):
        high, low = two_parts(vectors[8 * g : 8 * g + 8])
        both = jnp.concatenate([high, low], axis=0).astype(BF16)
        if transposed:
            both = jnp.concatenate([both, both], axis=1)
        total = jnp.zeros((8, TB), F32)
        for k in range(8):
            tile = split_ref[8 * g + k]
            if transposed:
                out = jnp.dot(both, tile, preferred_element_type=F32)
            else:
                out = lax.dot_general(
                    both, tile, (((1,), (1,)), ((), ())), preferred_element_type=F32
                )
                out = out[:, :TB] + out[:, TB:]
            total = jnp.where(sub == k, out[:8] + out[8:], total)
        groups.append(jnp.where(live[8 * g : 8 * g + 8] > 0.0, total, 0.0))
    return jnp.concatenate(groups, axis=0)


def split_tiles(tiles, split_ref, start, stop):
    for j in range(start, stop):
        high, low = two_parts(tiles[j])
        split_ref[j, :TB, :] = high.astype(BF16)
        split_ref[j, TB:, :] = low.astype(BF16)


def pick_rows(source, row_ref, picked):
    for j in range(CAP):
        picked[j : j + 1, :] = source[pl.ds(row_ref[j], 1), :]


def hits_of(wanted, lane_rows, width):
    pieces = [jnp.where(wanted == row, 1.0, 0.0) for row in lane_rows]
    return jnp.concatenate(pieces, axis=1)[:, :width].astype(BF16)


def index_row(index_ref, live, base):
    lane = iota((1, TB), 1)
    row = jnp.zeros((1, TB), F32)
    for j in range(CAP):
        value = jnp.where(j < live, index_ref[j] + 1, 0).astype(F32)
        row = jnp.where(lane == lax.rem(base + j, TB), value, row)
    return row


def index_lanes(in_ref, count):
    lane = iota((1, TB), 1)
    rows = []
    for k in range(-(-count * MSG // TB)):
        row = jnp.zeros((1, TB), F32)
        for i in range(count):
            low, high = MSG * i - TB * k, MSG * i + CAP - TB * k
            if high > 0 and low < TB:
                mine = (lane >= low) & (lane < high)
                row = jnp.where(mine, in_ref[MSG * i + CAP : MSG * (i + 1), :], row)
        rows.append(row)
    return rows


def send_to_all(out_ref, count, sums, row):
    message = jnp.concatenate([sums, row], axis=0)
    for i in range(count):
        out_ref[MSG * i : MSG * (i + 1), :] = message


def extra_sum(in_ref, count):
    row = in_ref[CAP : CAP + 1, :]
    for i in range(1, count):
        row = row + in_ref[MSG * i + CAP : MSG * (i + 1), :]
    return row


def scalar_row(rows):
    sums = jnp.sum(stack_rows(rows), axis=1, keepdims=True)
    apart = jnp.where(iota((EXTRA, TB), 0) == iota((EXTRA, TB), 1), sums, 0.0)
    return jnp.sum(apart, axis=0, keepdims=True)


def scalars_of(row, count):
    apart = jnp.where(iota((EXTRA, TB), 0) == iota((EXTRA, TB), 1), row, 0.0)
    sums = jnp.sum(apart, axis=1, keepdims=True)
    return [sums[k : k + 1] for k in range(count)]


def lane_sum(x):
    return jnp.sum(x, axis=0, keepdims=True)


def stack_rows(rows):
    sub = iota((EXTRA, TB), 0)
    out = jnp.zeros((EXTRA, TB), F32)
    for k, row in enumerate(rows):
        out = jnp.where(sub == k, row, out)
    return out


def first_kernel(
    row_hbm, col_hbm, live_hbm, tiles_hbm, scores_hbm, out_ref, info_ref,
    row_ref, col_ref, live_ref, tiles, scores, split_ref, picked, done,
):
    part = CAP // PARTS
    copies = [
        pltpu.make_async_copy(row_hbm, row_ref, done.at[0]),
        pltpu.make_async_copy(col_hbm, col_ref, done.at[1]),
        pltpu.make_async_copy(live_hbm, live_ref, done.at[2]),
        pltpu.make_async_copy(scores_hbm, scores, done.at[3]),
    ]
    for i in range(PARTS):
        some = pl.ds(part * i, part)
        copies.append(pltpu.make_async_copy(tiles_hbm.at[some], tiles.at[some], done.at[4 + i]))
    for copy in copies:
        copy.start()
    for copy in copies[:4]:
        copy.wait()
    live = live_ref[0]
    pick_rows(scores, row_ref, picked)
    far, _ = places()
    row = index_row(col_ref, live, slot_of(far, FAR_ORDER) * MSG)
    sub = iota((CAP, TB), 0)
    mask = jnp.where(sub < live, 1.0, 0.0)
    own = jnp.full((CAP, TB), -1.0, F32)
    for j in range(CAP):
        own = jnp.where(sub == j, jnp.where(j < live, row_ref[j] + 1, -1).astype(F32), own)
    place = slot_of(lax.axis_index("cols"), COL_ORDER)
    info_ref[:CAP, :] = mask
    info_ref[CAP : 2 * CAP, :] = own
    info_ref[2 * CAP :, :] = stack_rows([index_row(row_ref, live, place * MSG)])
    for i in range(PARTS):
        copies[4 + i].wait()
        split_tiles(tiles, split_ref, part * i, part * (i + 1))
    sums = times_tiles(picked[...], split_ref, mask, True)
    send_to_all(out_ref, FAR, sums, row)


def relay_kernel(in_ref, out_ref):
    rows = index_lanes(in_ref, FAR)
    for i in range(NEAR):
        out_ref[i, :LINE, :] = in_ref[...]
        out_ref[i, LINE:, :] = stack_rows(rows)


def send_forward(vectors, split_ref, info_ref, row, out_ref):
    send_to_all(out_ref, COLS, times_tiles(vectors, split_ref, info_ref[:CAP, :], False), row)


def gathered_kernel(
    info_ref, in_ref, tiles_ref, out_ref, gradient_ref, hits_ref, split_ref
):
    split_tiles(tiles_ref, split_ref, 0, CAP)
    far, near = places()
    slot = slot_of(far, FAR_ORDER)
    lines = -(-LINE // TB)
    index = [[in_ref[i, LINE + k : LINE + k + 1, :] for k in range(lines)] for i in range(NEAR)]
    own_rows = index[0]
    for i in range(1, NEAR):
        own_rows = [jnp.where(near == NEAR_ORDER[i], new, old) for new, old in zip(index[i], own_rows)]
    own_wanted = jnp.zeros((WANT, 1), F32)
    lane, sub = iota((CAP, TB), 1), iota((CAP, TB), 0)
    for i in range(NEAR):
        found = jnp.zeros((CAP, TB), F32)
        for k in range(lines):
            found = jnp.where(lane + k * TB == sub + slot * MSG, index[i][k], found)
        tile_part = jnp.sum(found, axis=1, keepdims=True)
        tile_part = jnp.where(tile_part == 0.0, -1.0, tile_part)
        share_part = ((far * NEAR + NEAR_ORDER[i]) * SHARE + 1 + iota((SHARE, 1), 0)).astype(F32)
        wanted = jnp.concatenate([tile_part, share_part], axis=0)
        hits_ref[WANT * i : WANT * (i + 1), :] = hits_of(wanted, own_rows, LINE)
        own_wanted = jnp.where(near == NEAR_ORDER[i], wanted, own_wanted)
    gradient = jnp.zeros((WANT, TB), F32)
    for i in range(NEAR):
        gradient += picked_sum(hits_of(own_wanted, index[i], LINE), in_ref[i, :LINE, :])
    gradient_ref[...] = gradient
    send_forward(gradient[:CAP], split_ref, info_ref, info_ref[2 * CAP : 2 * CAP + 1, :], out_ref)


def send_backward(picked, split_ref, info_ref, scalars, out_ref):
    sums = times_tiles(picked, split_ref, info_ref[:CAP, :], True)
    send_to_all(out_ref, FAR, sums, scalar_row(scalars))


def first_image_kernel(
    info_ref, in_ref, split_ref, scores_ref, out_ref, image_ref, hits_ref
):
    wanted = (iota((ROW_BLOCKS, 1), 0) + 1).astype(F32)
    wanted = jnp.concatenate([wanted, info_ref[CAP : 2 * CAP, :1]], axis=0)
    hits = hits_of(wanted, index_lanes(in_ref, COLS), SIDE)
    hits_ref[...] = hits
    sums = picked_sum(hits, in_ref[...])
    image = sums[:ROW_BLOCKS]
    image_ref[...] = image
    scalars = [lane_sum(image * scores_ref[...]), lane_sum(image * image)]
    send_backward(sums[ROW_BLOCKS:], split_ref, info_ref, scalars, out_ref)


def hand_kernel(in_ref, hits_ref, out_ref):
    extra = jnp.broadcast_to(extra_sum(in_ref, FAR), (EXTRA, TB))
    sums = picked_sum(hits_ref[...], in_ref[...])
    for i in range(NEAR):
        out_ref[i, :WANT, :] = sums[WANT * i : WANT * (i + 1)]
        out_ref[i, WANT:, :] = extra


def added(in_ref):
    total = in_ref[0]
    for i in range(1, in_ref.shape[0]):
        total = total + in_ref[i]
    return total


def second_gradient_kernel(
    info_ref, in_ref, split_ref, gradient_ref, out_ref, product_ref, next_ref, state_ref
):
    total = added(in_ref)
    product = total[:WANT]
    norm, image_norm = scalars_of(total[WANT : WANT + 1], 2)
    step = norm / image_norm
    following = gradient_ref[...] - step * product
    product_ref[...] = product
    next_ref[...] = following
    state_ref[...] = stack_rows([norm, image_norm, step])
    send_forward(following[:CAP], split_ref, info_ref, jnp.zeros((1, TB), F32), out_ref)


def second_image_kernel(
    info_ref, in_ref, split_ref, hits_ref, scores_ref, old_ref, state_ref, out_ref, image_ref
):
    sums = picked_sum(hits_ref[...], in_ref[...])
    image = sums[:ROW_BLOCKS]
    image_ref[...] = image
    old = old_ref[...]
    residual = scores_ref[...] - state_ref[2:3, :] * old
    scalars = [lane_sum(image * residual), lane_sum(image * image), lane_sum(image * old)]
    send_backward(sums[ROW_BLOCKS:], split_ref, info_ref, scalars, out_ref)


def third_gradient_kernel(
    info_ref, in_ref, split_ref, first_ref, second_ref, product_ref, state_ref,
    out_ref, keep_ref, later_ref,
):
    total = added(in_ref)
    old_norm, old_image_norm, old_step = state_ref[0:1, :], state_ref[1:2, :], state_ref[2:3, :]
    norm, straight, cross = scalars_of(total[WANT : WANT + 1], 3)
    ratio = norm / old_norm
    image_norm = straight + 2.0 * ratio * cross + ratio * ratio * old_image_norm
    step = norm / image_norm
    first, second = first_ref[...], second_ref[...]
    product = total[:WANT] + ratio * product_ref[...]
    third = second - step * product
    direction = second + ratio * first
    weights = old_step * first + step * direction
    keep_ref[0] = third[CAP:]
    keep_ref[1] = direction[CAP:]
    keep_ref[2] = weights[CAP:]
    later_ref[...] = stack_rows([norm, image_norm, step, ratio])
    send_forward(third[:CAP], split_ref, info_ref, jnp.zeros((1, TB), F32), out_ref)


def third_image_kernel(
    in_ref, hits_ref, scores_ref, first_ref, second_ref, state_ref, later_ref,
    out_ref, keep_ref,
):
    image = picked_sum(hits_ref[:ROW_BLOCKS, :], in_ref[...])
    first = first_ref[...]
    old = second_ref[...] + later_ref[3:4, :] * first
    residual = scores_ref[...] - state_ref[2:3, :] * first - later_ref[2:3, :] * old
    keep_ref[0] = image
    keep_ref[1] = old
    keep_ref[2] = residual
    scalars = [lane_sum(image * residual), lane_sum(image * image), lane_sum(image * old)]
    out_ref[...] = jnp.broadcast_to(scalar_row(scalars), (ROWS, TB))


def last_kernel(in_ref, keep_ref, image_ref, later_ref, weights_ref, residual_ref):
    norm, straight, cross = scalars_of(lane_sum(in_ref[...]), 3)
    ratio = norm / later_ref[0:1, :]
    image_norm = straight + 2.0 * ratio * cross + ratio * ratio * later_ref[1:2, :]
    step = norm / image_norm
    weights_ref[...] = keep_ref[2] + step * (keep_ref[0] + ratio * keep_ref[1])
    residual_ref[...] = image_ref[2] - step * (image_ref[0] + ratio * image_ref[1])


def call(kernel, outs, args, scratch=(), memory=None, room=16 * 2**20):
    def spec(x):
        scalar = x.dtype == jnp.int32
        return pl.BlockSpec(memory_space=memory or (pltpu.SMEM if scalar else pltpu.VMEM))

    return pl.pallas_call(
        kernel,
        out_shape=[jax.ShapeDtypeStruct(s, d) for s, d in outs],
        in_specs=[spec(a) for a in args],
        out_specs=[pl.BlockSpec(memory_space=pltpu.VMEM) for _ in outs],
        scratch_shapes=list(scratch),
        compiler_params=pltpu.CompilerParams(vmem_limit_bytes=room),
        name=kernel.__name__,
    )(*args)


GROUPS = {
    "far": [[far * NEAR + near for far in FAR_ORDER] for near in range(NEAR)],
    "near": [[far * NEAR + near for near in NEAR_ORDER] for far in range(FAR)],
    "rows": [[far * NEAR + near for far in FAR_ORDER for near in NEAR_ORDER]],
    "cols": [COL_ORDER],
}


def swap(x, kind, count):
    shape = x.shape
    if len(shape) == 2:
        x = x.reshape(count, shape[0] // count, 1, TB)
    axis, groups = "cols" if kind == "cols" else "rows", GROUPS[kind]
    return lax.all_to_all(x, axis, 0, 0, axis_index_groups=groups, tiled=True).reshape(shape)


def local(tiles, tile_row, tile_col, tile_counts, scores):
    f = lambda *shape: (shape, F32)
    b = lambda *shape: (shape, BF16)
    to_far, to_near = f(LINE, TB), f(NEAR, HAND, TB)
    to_cols = f(SIDE, TB)
    image_shape, state_shape = f(ROW_BLOCKS, TB), f(EXTRA, TB)

    message, info = call(
        first_kernel,
        [to_far, f(INFO, TB)],
        [tile_row, tile_col, tile_counts, tiles, scores],
        [
            pltpu.SMEM((CAP,), jnp.int32),
            pltpu.SMEM((CAP,), jnp.int32),
            pltpu.SMEM((1,), jnp.int32),
            pltpu.VMEM((CAP, TB, TB), F32),
            pltpu.VMEM((ROW_BLOCKS, TB), F32),
            pltpu.VMEM((CAP, 2 * TB, TB), BF16),
            pltpu.VMEM((CAP, TB), F32),
            pltpu.SemaphoreType.DMA((4 + PARTS,)),
        ],
        pltpu.HBM,
        62 * 2**20,
    )
    (message,) = call(relay_kernel, [f(NEAR, LINE + EXTRA, TB)], [swap(message, "far", FAR)])
    message, first, hand_hits, split = call(
        gathered_kernel,
        [to_cols, f(WANT, TB), b(NEAR * WANT, LINE), b(CAP, 2 * TB, TB)],
        [info, swap(message, "near", NEAR), tiles],
    )
    message, image, row_hits = call(
        first_image_kernel,
        [to_far, image_shape, b(ROW_BLOCKS + CAP, SIDE)],
        [info, swap(message, "cols", COLS), split, scores],
    )
    (message,) = call(hand_kernel, [to_near], [swap(message, "far", FAR), hand_hits])
    message, product, second, state = call(
        second_gradient_kernel,
        [to_cols, f(WANT, TB), f(WANT, TB), state_shape],
        [info, swap(message, "near", NEAR), split, first],
    )
    message, second_image = call(
        second_image_kernel,
        [to_far, image_shape],
        [info, swap(message, "cols", COLS), split, row_hits, scores, image, state],
    )
    (message,) = call(hand_kernel, [to_near], [swap(message, "far", FAR), hand_hits])
    message, keep, later = call(
        third_gradient_kernel,
        [to_cols, f(3, SHARE, TB), state_shape],
        [info, swap(message, "near", NEAR), split, first, second, product, state],
    )
    message, images = call(
        third_image_kernel,
        [f(ROWS, TB), f(3, ROW_BLOCKS, TB)],
        [swap(message, "cols", COLS), row_hits, scores, image, second_image, state, later],
    )
    weights, residual = call(
        last_kernel,
        [f(SHARE, TB), image_shape],
        [swap(message, "rows", ROWS), keep, images, later],
    )
    return weights, residual


def solution(mesh):
    every = ("rows", "cols")
    return jax.shard_map(
        local,
        mesh=mesh,
        in_specs=(P(every, None, None), P(every), P(every), P(every), P("rows", None)),
        out_specs=(P(("cols", "rows"), None), P("rows", None)),
        check_vma=False,
    )
```

```python
import functools

import jax
import jax.numpy as jnp
from jax import lax
from jax.experimental import pallas as pl
from jax.experimental.pallas import tpu as pltpu
from jax.sharding import PartitionSpec as P


FAR, NEAR, COLS = 8, 8, 8
ROWS = FAR * NEAR
FAR_ORDER = [4, 0, 1, 7, 2, 6, 3, 5]
NEAR_ORDER = [2, 3, 4, 5, 6, 7, 0, 1]
COL_ORDER = [5, 1, 7, 3, 4, 0, 6, 2]
CAP = 24
TB = 128
ROW_BLOCKS = 256
SHARE = 16
WANT = CAP + SHARE
EXTRA = 8
MSG = CAP + 1
LINE = FAR * MSG
SIDE = COLS * MSG
HAND = WANT + 1
PARTS = 3
INFO = 2 * CAP + EXTRA
F32 = jnp.float32
BF16 = jnp.bfloat16


def places():
    row = lax.axis_index("rows")
    return lax.div(row, NEAR), lax.rem(row, NEAR)


def slot_of(place, order):
    slot = 0
    for i, member in enumerate(order):
        slot = jnp.where(place == member, i, slot)
    return slot


def iota(shape, dim):
    return lax.broadcasted_iota(jnp.int32, shape, dim)


def two_parts(x):
    high = x.astype(BF16).astype(F32)
    return high, x - high


def side_by_side(x):
    high, low = two_parts(x)
    return jnp.concatenate([high, low], axis=1).astype(BF16)


def picked_sum(hits, values):
    out = jnp.dot(hits, side_by_side(values), preferred_element_type=F32)
    return out[:, :TB] + out[:, TB:]


def times_tiles(vectors, split_ref, live, transposed):
    sub = iota((8, TB), 0)
    groups = []
    for g in range(CAP // 8):
        high, low = two_parts(vectors[8 * g : 8 * g + 8])
        both = jnp.concatenate([high, low], axis=0).astype(BF16)
        if transposed:
            both = jnp.concatenate([both, both], axis=1)
        total = jnp.zeros((8, TB), F32)
        for k in range(8):
            tile = split_ref[8 * g + k]
            if transposed:
                out = jnp.dot(both, tile, preferred_element_type=F32)
            else:
                out = lax.dot_general(
                    both, tile, (((1,), (1,)), ((), ())), preferred_element_type=F32
                )
                out = out[:, :TB] + out[:, TB:]
            total = jnp.where(sub == k, out[:8] + out[8:], total)
        groups.append(jnp.where(live[8 * g : 8 * g + 8] > 0.0, total, 0.0))
    return jnp.concatenate(groups, axis=0)


def split_tiles(tiles, split_ref, start, stop):
    for j in range(start, stop):
        high, low = two_parts(tiles[j])
        split_ref[j, :TB, :] = high.astype(BF16)
        split_ref[j, TB:, :] = low.astype(BF16)


def pick_rows(source, row_ref, picked):
    for j in range(CAP):
        picked[j : j + 1, :] = source[pl.ds(row_ref[j], 1), :]


def hits_of(wanted, lane_rows, width):
    pieces = [jnp.where(wanted == row, 1.0, 0.0) for row in lane_rows]
    return jnp.concatenate(pieces, axis=1)[:, :width].astype(BF16)


def index_row(index_ref, live, base):
    lane = iota((1, TB), 1)
    row = jnp.zeros((1, TB), F32)
    for j in range(CAP):
        value = jnp.where(j < live, index_ref[j] + 1, 0).astype(F32)
        row = jnp.where(lane == lax.rem(base + j, TB), value, row)
    return row


def index_lanes(in_ref, count):
    lane = iota((1, TB), 1)
    rows = []
    for k in range(-(-count * MSG // TB)):
        row = jnp.zeros((1, TB), F32)
        for i in range(count):
            low, high = MSG * i - TB * k, MSG * i + CAP - TB * k
            if high > 0 and low < TB:
                mine = (lane >= low) & (lane < high)
                row = jnp.where(mine, in_ref[MSG * i + CAP : MSG * (i + 1), :], row)
        rows.append(row)
    return rows


def send_to_all(out_ref, count, sums, row):
    message = jnp.concatenate([sums, row], axis=0)
    for i in range(count):
        out_ref[MSG * i : MSG * (i + 1), :] = message


def extra_sum(in_ref, count):
    row = in_ref[CAP : CAP + 1, :]
    for i in range(1, count):
        row = row + in_ref[MSG * i + CAP : MSG * (i + 1), :]
    return row


def scalar_row(rows):
    sums = jnp.sum(stack_rows(rows), axis=1, keepdims=True)
    apart = jnp.where(iota((EXTRA, TB), 0) == iota((EXTRA, TB), 1), sums, 0.0)
    return jnp.sum(apart, axis=0, keepdims=True)


def scalars_of(row, count):
    apart = jnp.where(iota((EXTRA, TB), 0) == iota((EXTRA, TB), 1), row, 0.0)
    sums = jnp.sum(apart, axis=1, keepdims=True)
    return [sums[k : k + 1] for k in range(count)]


def lane_sum(x):
    return jnp.sum(x, axis=0, keepdims=True)


def stack_rows(rows):
    sub = iota((EXTRA, TB), 0)
    out = jnp.zeros((EXTRA, TB), F32)
    for k, row in enumerate(rows):
        out = jnp.where(sub == k, row, out)
    return out


def first_kernel(
    row_hbm, col_hbm, live_hbm, tiles_hbm, scores_hbm, out_ref, info_ref,
    row_ref, col_ref, live_ref, tiles, scores, split_ref, picked, done,
):
    part = CAP // PARTS
    copies = [
        pltpu.make_async_copy(row_hbm, row_ref, done.at[0]),
        pltpu.make_async_copy(col_hbm, col_ref, done.at[1]),
        pltpu.make_async_copy(live_hbm, live_ref, done.at[2]),
        pltpu.make_async_copy(scores_hbm, scores, done.at[3]),
    ]
    for i in range(PARTS):
        some = pl.ds(part * i, part)
        copies.append(pltpu.make_async_copy(tiles_hbm.at[some], tiles.at[some], done.at[4 + i]))
    for copy in copies:
        copy.start()
    for copy in copies[:4]:
        copy.wait()
    live = live_ref[0]
    pick_rows(scores, row_ref, picked)
    far, _ = places()
    row = index_row(col_ref, live, slot_of(far, FAR_ORDER) * MSG)
    sub = iota((CAP, TB), 0)
    mask = jnp.where(sub < live, 1.0, 0.0)
    own = jnp.full((CAP, TB), -1.0, F32)
    for j in range(CAP):
        own = jnp.where(sub == j, jnp.where(j < live, row_ref[j] + 1, -1).astype(F32), own)
    place = slot_of(lax.axis_index("cols"), COL_ORDER)
    info_ref[:CAP, :] = mask
    info_ref[CAP : 2 * CAP, :] = own
    info_ref[2 * CAP :, :] = stack_rows([index_row(row_ref, live, place * MSG)])
    for i in range(PARTS):
        copies[4 + i].wait()
        split_tiles(tiles, split_ref, part * i, part * (i + 1))
    sums = times_tiles(picked[...], split_ref, mask, True)
    send_to_all(out_ref, FAR, sums, row)


def relay_kernel(in_ref, out_ref):
    rows = index_lanes(in_ref, FAR)
    for i in range(NEAR):
        out_ref[i] = in_ref[...]
        for k, row in enumerate(rows):
            out_ref[i, MSG * k + CAP : MSG * (k + 1), :] = row


def send_forward(vectors, split_ref, info_ref, row, out_ref):
    send_to_all(out_ref, COLS, times_tiles(vectors, split_ref, info_ref[:CAP, :], False), row)


def gathered_kernel(
    info_ref, in_ref, tiles_ref, out_ref, gradient_ref, hits_ref, split_ref
):
    split_tiles(tiles_ref, split_ref, 0, CAP)
    far, near = places()
    slot = slot_of(far, FAR_ORDER)
    lines = -(-LINE // TB)
    index = [
        [in_ref[i, MSG * k + CAP : MSG * (k + 1), :] for k in range(lines)] for i in range(NEAR)
    ]
    own_rows = index[0]
    for i in range(1, NEAR):
        own_rows = [jnp.where(near == NEAR_ORDER[i], new, old) for new, old in zip(index[i], own_rows)]
    own_wanted = jnp.zeros((WANT, 1), F32)
    every_wanted = []
    lane, sub = iota((CAP, TB), 1), iota((CAP, TB), 0)
    for i in range(NEAR):
        found = jnp.zeros((CAP, TB), F32)
        for k in range(lines):
            found = jnp.where(lane + k * TB == sub + slot * MSG, index[i][k], found)
        tile_part = jnp.sum(found, axis=1, keepdims=True)
        tile_part = jnp.where(tile_part == 0.0, -1.0, tile_part)
        share_part = ((far * NEAR + NEAR_ORDER[i]) * SHARE + 1 + iota((SHARE, 1), 0)).astype(F32)
        wanted = jnp.concatenate([tile_part, share_part], axis=0)
        every_wanted.append(wanted)
        own_wanted = jnp.where(near == NEAR_ORDER[i], wanted, own_wanted)
    hits_ref[...] = hits_of(jnp.concatenate(every_wanted, axis=0), own_rows, LINE)
    gradient = jnp.zeros((WANT, TB), F32)
    for i in range(NEAR):
        gradient += picked_sum(hits_of(own_wanted, index[i], LINE), in_ref[i])
    gradient_ref[...] = gradient
    send_forward(gradient[:CAP], split_ref, info_ref, info_ref[2 * CAP : 2 * CAP + 1, :], out_ref)


def send_backward(picked, split_ref, info_ref, scalars, out_ref):
    sums = times_tiles(picked, split_ref, info_ref[:CAP, :], True)
    send_to_all(out_ref, FAR, sums, scalar_row(scalars))


def first_image_kernel(
    info_ref, in_ref, split_ref, scores_ref, out_ref, image_ref, hits_ref
):
    wanted = (iota((ROW_BLOCKS, 1), 0) + 1).astype(F32)
    wanted = jnp.concatenate([wanted, info_ref[CAP : 2 * CAP, :1]], axis=0)
    hits = hits_of(wanted, index_lanes(in_ref, COLS), SIDE)
    hits_ref[...] = hits
    sums = picked_sum(hits, in_ref[...])
    image = sums[:ROW_BLOCKS]
    image_ref[...] = image
    scalars = [lane_sum(image * scores_ref[...]), lane_sum(image * image)]
    send_backward(sums[ROW_BLOCKS:], split_ref, info_ref, scalars, out_ref)


def hand_kernel(in_ref, hits_ref, out_ref):
    extra = extra_sum(in_ref, FAR)
    sums = picked_sum(hits_ref[...], in_ref[...])
    for i in range(NEAR):
        some = jnp.concatenate([sums[WANT * i : WANT * (i + 1)], extra], axis=0)
        out_ref[HAND * i : HAND * (i + 1), :] = some


def added(in_ref):
    total = in_ref[:HAND, :]
    for i in range(1, NEAR):
        total = total + in_ref[HAND * i : HAND * (i + 1), :]
    return total


def second_gradient_kernel(
    info_ref, in_ref, split_ref, gradient_ref, out_ref, product_ref, next_ref, state_ref
):
    total = added(in_ref)
    product = total[:WANT]
    norm, image_norm = scalars_of(total[WANT : WANT + 1], 2)
    step = norm / image_norm
    following = gradient_ref[...] - step * product
    product_ref[...] = product
    next_ref[...] = following
    state_ref[...] = stack_rows([norm, image_norm, step])
    send_forward(following[:CAP], split_ref, info_ref, jnp.zeros((1, TB), F32), out_ref)


def second_image_kernel(
    info_ref, in_ref, split_ref, hits_ref, scores_ref, old_ref, state_ref, out_ref, image_ref
):
    sums = picked_sum(hits_ref[...], in_ref[...])
    image = sums[:ROW_BLOCKS]
    image_ref[...] = image
    old = old_ref[...]
    residual = scores_ref[...] - state_ref[2:3, :] * old
    scalars = [lane_sum(image * residual), lane_sum(image * image), lane_sum(image * old)]
    send_backward(sums[ROW_BLOCKS:], split_ref, info_ref, scalars, out_ref)


def third_gradient_kernel(
    info_ref, in_ref, split_ref, first_ref, second_ref, product_ref, state_ref,
    out_ref, keep_ref, later_ref,
):
    total = added(in_ref)
    old_norm, old_image_norm, old_step = state_ref[0:1, :], state_ref[1:2, :], state_ref[2:3, :]
    norm, straight, cross = scalars_of(total[WANT : WANT + 1], 3)
    ratio = norm / old_norm
    image_norm = straight + 2.0 * ratio * cross + ratio * ratio * old_image_norm
    step = norm / image_norm
    first, second = first_ref[...], second_ref[...]
    product = total[:WANT] + ratio * product_ref[...]
    third = second - step * product
    direction = second + ratio * first
    weights = old_step * first + step * direction
    keep_ref[0] = third[CAP:]
    keep_ref[1] = direction[CAP:]
    keep_ref[2] = weights[CAP:]
    later_ref[...] = stack_rows([norm, image_norm, step, ratio])
    send_forward(third[:CAP], split_ref, info_ref, jnp.zeros((1, TB), F32), out_ref)


def third_image_kernel(
    in_ref, hits_ref, scores_ref, first_ref, second_ref, state_ref, later_ref,
    out_ref, keep_ref,
):
    image = picked_sum(hits_ref[:ROW_BLOCKS, :], in_ref[...])
    first = first_ref[...]
    old = second_ref[...] + later_ref[3:4, :] * first
    residual = scores_ref[...] - state_ref[2:3, :] * first - later_ref[2:3, :] * old
    keep_ref[0] = image
    keep_ref[1] = old
    keep_ref[2] = residual
    scalars = [lane_sum(image * residual), lane_sum(image * image), lane_sum(image * old)]
    out_ref[...] = jnp.broadcast_to(scalar_row(scalars), (ROWS, TB))


def last_kernel(in_ref, keep_ref, image_ref, later_ref, weights_ref, residual_ref):
    norm, straight, cross = scalars_of(lane_sum(in_ref[...]), 3)
    ratio = norm / later_ref[0:1, :]
    image_norm = straight + 2.0 * ratio * cross + ratio * ratio * later_ref[1:2, :]
    step = norm / image_norm
    weights_ref[...] = keep_ref[2] + step * (keep_ref[0] + ratio * keep_ref[1])
    residual_ref[...] = image_ref[2] - step * (image_ref[0] + ratio * image_ref[1])


def call(kernel, outs, args, scratch=(), memory=None, room=16 * 2**20):
    def spec(x):
        scalar = x.dtype == jnp.int32
        return pl.BlockSpec(memory_space=memory or (pltpu.SMEM if scalar else pltpu.VMEM))

    return pl.pallas_call(
        kernel,
        out_shape=[jax.ShapeDtypeStruct(s, d) for s, d in outs],
        in_specs=[spec(a) for a in args],
        out_specs=[pl.BlockSpec(memory_space=pltpu.VMEM) for _ in outs],
        scratch_shapes=list(scratch),
        compiler_params=pltpu.CompilerParams(vmem_limit_bytes=room),
        name=kernel.__name__,
    )(*args)


GROUPS = {
    "far": [[far * NEAR + near for far in FAR_ORDER] for near in range(NEAR)],
    "near": [[far * NEAR + near for near in NEAR_ORDER] for far in range(FAR)],
    "rows": [[far * NEAR + near for far in FAR_ORDER for near in NEAR_ORDER]],
    "cols": [COL_ORDER],
}


def swap(x, kind, count):
    shape = x.shape
    if len(shape) == 2:
        x = x.reshape(count, shape[0] // count, 1, TB)
    axis, groups = "cols" if kind == "cols" else "rows", GROUPS[kind]
    return lax.all_to_all(x, axis, 0, 0, axis_index_groups=groups, tiled=True).reshape(shape)


def local(tiles, tile_row, tile_col, tile_counts, scores):
    f = lambda *shape: (shape, F32)
    b = lambda *shape: (shape, BF16)
    to_far, to_near = f(LINE, TB), f(NEAR * HAND, TB)
    to_cols = f(SIDE, TB)
    image_shape, state_shape = f(ROW_BLOCKS, TB), f(EXTRA, TB)

    message, info = call(
        first_kernel,
        [to_far, f(INFO, TB)],
        [tile_row, tile_col, tile_counts, tiles, scores],
        [
            pltpu.SMEM((CAP,), jnp.int32),
            pltpu.SMEM((CAP,), jnp.int32),
            pltpu.SMEM((1,), jnp.int32),
            pltpu.VMEM((CAP, TB, TB), F32),
            pltpu.VMEM((ROW_BLOCKS, TB), F32),
            pltpu.VMEM((CAP, 2 * TB, TB), BF16),
            pltpu.VMEM((CAP, TB), F32),
            pltpu.SemaphoreType.DMA((4 + PARTS,)),
        ],
        pltpu.HBM,
        62 * 2**20,
    )
    (message,) = call(relay_kernel, [f(NEAR, LINE, TB)], [swap(message, "far", FAR)])
    message, first, hand_hits, split = call(
        gathered_kernel,
        [to_cols, f(WANT, TB), b(NEAR * WANT, LINE), b(CAP, 2 * TB, TB)],
        [info, swap(message, "near", NEAR), tiles],
    )
    message, image, row_hits = call(
        first_image_kernel,
        [to_far, image_shape, b(ROW_BLOCKS + CAP, SIDE)],
        [info, swap(message, "cols", COLS), split, scores],
    )
    (message,) = call(hand_kernel, [to_near], [swap(message, "far", FAR), hand_hits])
    message, product, second, state = call(
        second_gradient_kernel,
        [to_cols, f(WANT, TB), f(WANT, TB), state_shape],
        [info, swap(message, "near", NEAR), split, first],
    )
    message, second_image = call(
        second_image_kernel,
        [to_far, image_shape],
        [info, swap(message, "cols", COLS), split, row_hits, scores, image, state],
    )
    (message,) = call(hand_kernel, [to_near], [swap(message, "far", FAR), hand_hits])
    message, keep, later = call(
        third_gradient_kernel,
        [to_cols, f(3, SHARE, TB), state_shape],
        [info, swap(message, "near", NEAR), split, first, second, product, state],
    )
    message, images = call(
        third_image_kernel,
        [f(ROWS, TB), f(3, ROW_BLOCKS, TB)],
        [swap(message, "cols", COLS), row_hits, scores, image, second_image, state, later],
    )
    weights, residual = call(
        last_kernel,
        [f(SHARE, TB), image_shape],
        [swap(message, "rows", ROWS), keep, images, later],
    )
    return weights, residual


def solution(mesh):
    every = ("rows", "cols")
    return jax.shard_map(
        local,
        mesh=mesh,
        in_specs=(P(every, None, None), P(every), P(every), P(every), P("rows", None)),
        out_specs=(P(("cols", "rows"), None), P("rows", None)),
        check_vma=False,
    )
```

```python
import functools

import jax
import jax.numpy as jnp
from jax import lax
from jax.experimental import pallas as pl
from jax.experimental.pallas import tpu as pltpu
from jax.sharding import PartitionSpec as P


FAR, NEAR, COLS = 8, 8, 8
ROWS = FAR * NEAR
FAR_ORDERS = [[4, 0, 1, 7, 2, 6, 3, 5], [4, 0, 7, 1, 6, 2, 5, 3]]
NEAR_ORDER = [2, 3, 4, 5, 6, 7, 0, 1]
COL_ORDER = [5, 1, 7, 3, 4, 0, 6, 2]
CAP = 24
TB = 128
ROW_BLOCKS = 256
SHARE = 16
WANT = CAP + SHARE
EXTRA = 8
MSG = CAP + 1
LINE = FAR * MSG
SIDE = COLS * MSG
HAND = WANT + 1
PARTS = CAP // 8
INFO = 2 * CAP + EXTRA
F32 = jnp.float32
BF16 = jnp.bfloat16


def places():
    row = lax.axis_index("rows")
    return lax.div(row, NEAR), lax.rem(row, NEAR)


def slot_of(place, order):
    slot = 0
    for i, member in enumerate(order):
        slot = jnp.where(place == member, i, slot)
    return slot


def far_slot(far):
    first, second = [slot_of(far, order) for order in FAR_ORDERS]
    return jnp.where(lax.rem(lax.axis_index("cols"), 2) == 0, first, second)


def iota(shape, dim):
    return lax.broadcasted_iota(jnp.int32, shape, dim)


def two_parts(x):
    high = x.astype(BF16).astype(F32)
    return high, x - high


def side_by_side(x):
    high, low = two_parts(x)
    return jnp.concatenate([high, low], axis=1).astype(BF16)


def picked_sum(hits, values):
    out = jnp.dot(hits, side_by_side(values), preferred_element_type=F32)
    return out[:, :TB] + out[:, TB:]


def times_group(g, vectors, split_ref, live, transposed):
    sub = iota((8, TB), 0)
    high, low = two_parts(vectors[8 * g : 8 * g + 8])
    both = jnp.concatenate([high, low], axis=0).astype(BF16)
    if transposed:
        both = jnp.concatenate([both, both], axis=1)
    total = jnp.zeros((8, TB), F32)
    for k in range(8):
        tile = split_ref[8 * g + k]
        if transposed:
            out = jnp.dot(both, tile, preferred_element_type=F32)
        else:
            out = lax.dot_general(both, tile, (((1,), (1,)), ((), ())), preferred_element_type=F32)
            out = out[:, :TB] + out[:, TB:]
        total = jnp.where(sub == k, out[:8] + out[8:], total)
    return jnp.where(live[8 * g : 8 * g + 8] > 0.0, total, 0.0)


def times_tiles(vectors, split_ref, live, transposed):
    groups = [times_group(g, vectors, split_ref, live, transposed) for g in range(CAP // 8)]
    return jnp.concatenate(groups, axis=0)


def split_tiles(tiles, split_ref, start, stop):
    for j in range(start, stop):
        high, low = two_parts(tiles[j])
        split_ref[j, :TB, :] = high.astype(BF16)
        split_ref[j, TB:, :] = low.astype(BF16)


def pick_rows(source, row_ref, picked):
    for j in range(CAP):
        picked[j : j + 1, :] = source[pl.ds(row_ref[j], 1), :]


def hits_of(wanted, lane_rows, width):
    pieces = [jnp.where(wanted == row, 1.0, 0.0) for row in lane_rows]
    return jnp.concatenate(pieces, axis=1)[:, :width].astype(BF16)


def index_row(index_ref, live, base):
    lane = iota((1, TB), 1)
    row = jnp.zeros((1, TB), F32)
    for j in range(CAP):
        value = jnp.where(j < live, index_ref[j] + 1, 0).astype(F32)
        row = jnp.where(lane == lax.rem(base + j, TB), value, row)
    return row


def index_lanes(in_ref, count):
    lane = iota((1, TB), 1)
    rows = []
    for k in range(-(-count * MSG // TB)):
        row = jnp.zeros((1, TB), F32)
        for i in range(count):
            low, high = MSG * i - TB * k, MSG * i + CAP - TB * k
            if high > 0 and low < TB:
                mine = (lane >= low) & (lane < high)
                row = jnp.where(mine, in_ref[MSG * i + CAP : MSG * (i + 1), :], row)
        rows.append(row)
    return rows


def send_to_all(out_ref, count, sums, row):
    message = jnp.concatenate([sums, row], axis=0)
    for i in range(count):
        out_ref[MSG * i : MSG * (i + 1), :] = message


def extra_sum(in_ref, count):
    row = in_ref[CAP : CAP + 1, :]
    for i in range(1, count):
        row = row + in_ref[MSG * i + CAP : MSG * (i + 1), :]
    return row


def scalar_row(rows):
    sums = jnp.sum(stack_rows(rows), axis=1, keepdims=True)
    apart = jnp.where(iota((EXTRA, TB), 0) == iota((EXTRA, TB), 1), sums, 0.0)
    return jnp.sum(apart, axis=0, keepdims=True)


def scalars_of(row, count):
    apart = jnp.where(iota((EXTRA, TB), 0) == iota((EXTRA, TB), 1), row, 0.0)
    sums = jnp.sum(apart, axis=1, keepdims=True)
    return [sums[k : k + 1] for k in range(count)]


def lane_sum(x):
    return jnp.sum(x, axis=0, keepdims=True)


def stack_rows(rows):
    sub = iota((EXTRA, TB), 0)
    out = jnp.zeros((EXTRA, TB), F32)
    for k, row in enumerate(rows):
        out = jnp.where(sub == k, row, out)
    return out


def first_kernel(
    row_hbm, col_hbm, live_hbm, tiles_hbm, scores_hbm, out_ref, info_ref,
    row_ref, col_ref, live_ref, tiles, scores, split_ref, picked, done,
):
    part = CAP // PARTS
    copies = [
        pltpu.make_async_copy(row_hbm, row_ref, done.at[0]),
        pltpu.make_async_copy(col_hbm, col_ref, done.at[1]),
        pltpu.make_async_copy(live_hbm, live_ref, done.at[2]),
        pltpu.make_async_copy(scores_hbm, scores, done.at[3]),
    ]
    for i in range(PARTS):
        some = pl.ds(part * i, part)
        copies.append(pltpu.make_async_copy(tiles_hbm.at[some], tiles.at[some], done.at[4 + i]))
    for copy in copies:
        copy.start()
    for copy in copies[:4]:
        copy.wait()
    live = live_ref[0]
    pick_rows(scores, row_ref, picked)
    far, _ = places()
    row = index_row(col_ref, live, far_slot(far) * MSG)
    sub = iota((CAP, TB), 0)
    mask = jnp.where(sub < live, 1.0, 0.0)
    own = jnp.full((CAP, TB), -1.0, F32)
    for j in range(CAP):
        own = jnp.where(sub == j, jnp.where(j < live, row_ref[j] + 1, -1).astype(F32), own)
    place = slot_of(lax.axis_index("cols"), COL_ORDER)
    info_ref[:CAP, :] = mask
    info_ref[CAP : 2 * CAP, :] = own
    info_ref[2 * CAP :, :] = stack_rows([index_row(row_ref, live, place * MSG)])
    groups, rows = [], picked[...]
    for i in range(PARTS):
        copies[4 + i].wait()
        split_tiles(tiles, split_ref, part * i, part * (i + 1))
        groups.append(times_group(i, rows, split_ref, mask, True))
    sums = jnp.concatenate(groups, axis=0)
    send_to_all(out_ref, FAR, sums, row)


def relay_kernel(in_ref, out_ref):
    rows = index_lanes(in_ref, FAR)
    for i in range(NEAR):
        out_ref[i] = in_ref[...]
        for k, row in enumerate(rows):
            out_ref[i, MSG * k + CAP : MSG * (k + 1), :] = row


def forward(vectors, split_ref, info_ref):
    return times_tiles(vectors[:CAP], split_ref, info_ref[:CAP, :], False)


def gathered_kernel(
    info_ref, in_ref, tiles_ref, out_ref, gradient_ref, hits_ref, split_ref, sums_ref
):
    split_tiles(tiles_ref, split_ref, 0, CAP)
    far, near = places()
    slot = far_slot(far)
    lines = -(-LINE // TB)
    index = [
        [in_ref[i, MSG * k + CAP : MSG * (k + 1), :] for k in range(lines)] for i in range(NEAR)
    ]
    own_rows = index[0]
    for i in range(1, NEAR):
        own_rows = [jnp.where(near == NEAR_ORDER[i], new, old) for new, old in zip(index[i], own_rows)]
    own_wanted = jnp.zeros((WANT, 1), F32)
    every_wanted = []
    lane, sub = iota((CAP, TB), 1), iota((CAP, TB), 0)
    for i in range(NEAR):
        found = jnp.zeros((CAP, TB), F32)
        for k in range(lines):
            found = jnp.where(lane + k * TB == sub + slot * MSG, index[i][k], found)
        tile_part = jnp.sum(found, axis=1, keepdims=True)
        tile_part = jnp.where(tile_part == 0.0, -1.0, tile_part)
        share_part = ((far * NEAR + NEAR_ORDER[i]) * SHARE + 1 + iota((SHARE, 1), 0)).astype(F32)
        wanted = jnp.concatenate([tile_part, share_part], axis=0)
        every_wanted.append(wanted)
        own_wanted = jnp.where(near == NEAR_ORDER[i], wanted, own_wanted)
    hits_ref[...] = hits_of(jnp.concatenate(every_wanted, axis=0), own_rows, LINE)
    gradient = jnp.zeros((WANT, TB), F32)
    for i in range(NEAR):
        gradient += picked_sum(hits_of(own_wanted, index[i], LINE), in_ref[i])
    gradient_ref[...] = gradient
    sums = forward(gradient, split_ref, info_ref)
    sums_ref[...] = sums
    send_to_all(out_ref, COLS, sums, info_ref[2 * CAP : 2 * CAP + 1, :])


def send_backward(picked, split_ref, info_ref, scalars, out_ref):
    sums = times_tiles(picked, split_ref, info_ref[:CAP, :], True)
    send_to_all(out_ref, FAR, sums, scalar_row(scalars))


def first_image_kernel(
    info_ref, in_ref, split_ref, scores_ref, out_ref, image_ref, hits_ref
):
    wanted = (iota((ROW_BLOCKS, 1), 0) + 1).astype(F32)
    wanted = jnp.concatenate([wanted, info_ref[CAP : 2 * CAP, :1]], axis=0)
    hits = hits_of(wanted, index_lanes(in_ref, COLS), SIDE)
    hits_ref[...] = hits
    sums = picked_sum(hits, in_ref[...])
    image = sums[:ROW_BLOCKS]
    image_ref[...] = image
    scalars = [lane_sum(image * scores_ref[...]), lane_sum(image * image)]
    send_backward(sums[ROW_BLOCKS:], split_ref, info_ref, scalars, out_ref)


def hand_kernel(in_ref, hits_ref, out_ref):
    extra = extra_sum(in_ref, FAR)
    sums = picked_sum(hits_ref[...], in_ref[...])
    for i in range(NEAR):
        some = jnp.concatenate([sums[WANT * i : WANT * (i + 1)], extra], axis=0)
        out_ref[HAND * i : HAND * (i + 1), :] = some


def added(in_ref):
    total = in_ref[:HAND, :]
    for i in range(1, NEAR):
        total = total + in_ref[HAND * i : HAND * (i + 1), :]
    return total


def second_gradient_kernel(
    info_ref, in_ref, split_ref, gradient_ref, sums_ref,
    out_ref, product_ref, next_ref, state_ref, product_sums_ref, next_sums_ref,
):
    total = added(in_ref)
    product = total[:WANT]
    product_sums = forward(product, split_ref, info_ref)
    product_sums_ref[...] = product_sums
    norm, image_norm = scalars_of(total[WANT : WANT + 1], 2)
    step = norm / image_norm
    following = gradient_ref[...] - step * product
    product_ref[...] = product
    next_ref[...] = following
    state_ref[...] = stack_rows([norm, image_norm, step])
    next_sums = sums_ref[...] - step * product_sums
    next_sums_ref[...] = next_sums
    send_to_all(out_ref, COLS, next_sums, jnp.zeros((1, TB), F32))


def second_image_kernel(
    info_ref, in_ref, split_ref, hits_ref, scores_ref, old_ref, state_ref, out_ref, image_ref
):
    sums = picked_sum(hits_ref[...], in_ref[...])
    image = sums[:ROW_BLOCKS]
    image_ref[...] = image
    old = old_ref[...]
    residual = scores_ref[...] - state_ref[2:3, :] * old
    scalars = [lane_sum(image * residual), lane_sum(image * image), lane_sum(image * old)]
    send_backward(sums[ROW_BLOCKS:], split_ref, info_ref, scalars, out_ref)


def third_gradient_kernel(
    info_ref, in_ref, split_ref, first_ref, second_ref, product_ref, state_ref,
    product_sums_ref, second_sums_ref, out_ref, keep_ref, later_ref,
):
    total = added(in_ref)
    product_sums = forward(total, split_ref, info_ref)
    old_norm, old_image_norm, old_step = state_ref[0:1, :], state_ref[1:2, :], state_ref[2:3, :]
    norm, straight, cross = scalars_of(total[WANT : WANT + 1], 3)
    ratio = norm / old_norm
    image_norm = straight + 2.0 * ratio * cross + ratio * ratio * old_image_norm
    step = norm / image_norm
    first, second = first_ref[...], second_ref[...]
    product = total[:WANT] + ratio * product_ref[...]
    third = second - step * product
    direction = second + ratio * first
    weights = old_step * first + step * direction
    keep_ref[0] = third[CAP:]
    keep_ref[1] = direction[CAP:]
    keep_ref[2] = weights[CAP:]
    later_ref[...] = stack_rows([norm, image_norm, step, ratio])
    product_sums = product_sums + ratio * product_sums_ref[...]
    send_to_all(out_ref, COLS, second_sums_ref[...] - step * product_sums, jnp.zeros((1, TB), F32))


def third_image_kernel(
    in_ref, hits_ref, scores_ref, first_ref, second_ref, state_ref, later_ref,
    out_ref, keep_ref,
):
    image = picked_sum(hits_ref[:ROW_BLOCKS, :], in_ref[...])
    first = first_ref[...]
    old = second_ref[...] + later_ref[3:4, :] * first
    residual = scores_ref[...] - state_ref[2:3, :] * first - later_ref[2:3, :] * old
    keep_ref[0] = image
    keep_ref[1] = old
    keep_ref[2] = residual
    scalars = [lane_sum(image * residual), lane_sum(image * image), lane_sum(image * old)]
    out_ref[...] = jnp.broadcast_to(scalar_row(scalars), (ROWS, TB))


def last_kernel(in_ref, keep_ref, image_ref, later_ref, weights_ref, residual_ref):
    norm, straight, cross = scalars_of(lane_sum(in_ref[...]), 3)
    ratio = norm / later_ref[0:1, :]
    image_norm = straight + 2.0 * ratio * cross + ratio * ratio * later_ref[1:2, :]
    step = norm / image_norm
    weights_ref[...] = keep_ref[2] + step * (keep_ref[0] + ratio * keep_ref[1])
    residual_ref[...] = image_ref[2] - step * (image_ref[0] + ratio * image_ref[1])


def call(kernel, outs, args, scratch=(), memory=None, room=16 * 2**20):
    def spec(x):
        scalar = x.dtype == jnp.int32
        return pl.BlockSpec(memory_space=memory or (pltpu.SMEM if scalar else pltpu.VMEM))

    return pl.pallas_call(
        kernel,
        out_shape=[jax.ShapeDtypeStruct(s, d) for s, d in outs],
        in_specs=[spec(a) for a in args],
        out_specs=[pl.BlockSpec(memory_space=pltpu.VMEM) for _ in outs],
        scratch_shapes=list(scratch),
        compiler_params=pltpu.CompilerParams(vmem_limit_bytes=room),
        name=kernel.__name__,
    )(*args)


GROUPS = {
    "far": [
        [(far * NEAR + near) * COLS + col for far in FAR_ORDERS[col % 2]]
        for near in range(NEAR)
        for col in range(COLS)
    ],
    "near": [[far * NEAR + near for near in NEAR_ORDER] for far in range(FAR)],
    "rows": [[far * NEAR + near for far in FAR_ORDERS[0] for near in NEAR_ORDER]],
    "cols": [COL_ORDER],
}


def swap(x, kind, count):
    shape = x.shape
    if len(shape) == 2:
        x = x.reshape(count, shape[0] // count, 1, TB)
    axis = {"cols": "cols", "far": ("rows", "cols")}.get(kind, "rows")
    groups = GROUPS[kind]
    return lax.all_to_all(x, axis, 0, 0, axis_index_groups=groups, tiled=True).reshape(shape)


def local(tiles, tile_row, tile_col, tile_counts, scores):
    f = lambda *shape: (shape, F32)
    b = lambda *shape: (shape, BF16)
    to_far, to_near = f(LINE, TB), f(NEAR * HAND, TB)
    to_cols = f(SIDE, TB)
    own = f(CAP, TB)
    image_shape, state_shape = f(ROW_BLOCKS, TB), f(EXTRA, TB)

    message, info = call(
        first_kernel,
        [to_far, f(INFO, TB)],
        [tile_row, tile_col, tile_counts, tiles, scores],
        [
            pltpu.SMEM((CAP,), jnp.int32),
            pltpu.SMEM((CAP,), jnp.int32),
            pltpu.SMEM((1,), jnp.int32),
            pltpu.VMEM((CAP, TB, TB), F32),
            pltpu.VMEM((ROW_BLOCKS, TB), F32),
            pltpu.VMEM((CAP, 2 * TB, TB), BF16),
            pltpu.VMEM((CAP, TB), F32),
            pltpu.SemaphoreType.DMA((4 + PARTS,)),
        ],
        pltpu.HBM,
        62 * 2**20,
    )
    (message,) = call(relay_kernel, [f(NEAR, LINE, TB)], [swap(message, "far", FAR)])
    message, first, hand_hits, split, first_sums = call(
        gathered_kernel,
        [to_cols, f(WANT, TB), b(NEAR * WANT, LINE), b(CAP, 2 * TB, TB), own],
        [info, swap(message, "near", NEAR), tiles],
    )
    message, image, row_hits = call(
        first_image_kernel,
        [to_far, image_shape, b(ROW_BLOCKS + CAP, SIDE)],
        [info, swap(message, "cols", COLS), split, scores],
    )
    (message,) = call(hand_kernel, [to_near], [swap(message, "far", FAR), hand_hits])
    message, product, second, state, product_sums, second_sums = call(
        second_gradient_kernel,
        [to_cols, f(WANT, TB), f(WANT, TB), state_shape, own, own],
        [info, swap(message, "near", NEAR), split, first, first_sums],
    )
    message, second_image = call(
        second_image_kernel,
        [to_far, image_shape],
        [info, swap(message, "cols", COLS), split, row_hits, scores, image, state],
    )
    (message,) = call(hand_kernel, [to_near], [swap(message, "far", FAR), hand_hits])
    message, keep, later = call(
        third_gradient_kernel,
        [to_cols, f(3, SHARE, TB), state_shape],
        [
            info, swap(message, "near", NEAR), split, first, second, product, state,
            product_sums, second_sums,
        ],
    )
    message, images = call(
        third_image_kernel,
        [f(ROWS, TB), f(3, ROW_BLOCKS, TB)],
        [swap(message, "cols", COLS), row_hits, scores, image, second_image, state, later],
    )
    weights, residual = call(
        last_kernel,
        [f(SHARE, TB), image_shape],
        [swap(message, "rows", ROWS), keep, images, later],
    )
    return weights, residual


def solution(mesh):
    every = ("rows", "cols")
    return jax.shard_map(
        local,
        mesh=mesh,
        in_specs=(P(every, None, None), P(every), P(every), P(every), P("rows", None)),
        out_specs=(P(("cols", "rows"), None), P("rows", None)),
        check_vma=False,
    )
```

```python
import functools

import jax
import jax.numpy as jnp
from jax import lax
from jax.experimental import pallas as pl
from jax.experimental.pallas import tpu as pltpu
from jax.sharding import PartitionSpec as P


FAR, NEAR, COLS = 8, 8, 8
ROWS = FAR * NEAR
FAR_ORDERS = [[4, 0, 1, 7, 2, 6, 3, 5], [4, 0, 7, 1, 6, 2, 5, 3]]
NEAR_ORDER = [2, 3, 4, 5, 6, 7, 0, 1]
COL_ORDER = [5, 1, 7, 3, 4, 0, 6, 2]
CAP = 24
TB = 128
ROW_BLOCKS = 256
SHARE = 16
WANT = CAP + SHARE
EXTRA = 8
MSG = CAP + 1
LINE = FAR * MSG
SIDE = COLS * MSG
HAND = WANT + 1
PARTS = CAP // 8
INFO = 2 * CAP + EXTRA
F32 = jnp.float32
BF16 = jnp.bfloat16


def places():
    row = lax.axis_index("rows")
    return lax.div(row, NEAR), lax.rem(row, NEAR)


def slot_of(place, order):
    slot = 0
    for i, member in enumerate(order):
        slot = jnp.where(place == member, i, slot)
    return slot


def far_slot(far):
    first, second = [slot_of(far, order) for order in FAR_ORDERS]
    return jnp.where(lax.rem(lax.axis_index("cols"), 2) == 0, first, second)


def iota(shape, dim):
    return lax.broadcasted_iota(jnp.int32, shape, dim)


def two_parts(x):
    high = x.astype(BF16).astype(F32)
    return high, x - high


def side_by_side(x):
    high, low = two_parts(x)
    return jnp.concatenate([high, low], axis=1).astype(BF16)


def picked_sum(hits, values):
    out = jnp.dot(hits, side_by_side(values), preferred_element_type=F32)
    return out[:, :TB] + out[:, TB:]


def times_group(g, vectors, split_ref, live, transposed):
    sub = iota((8, TB), 0)
    high, low = two_parts(vectors[8 * g : 8 * g + 8])
    both = jnp.concatenate([high, low], axis=0).astype(BF16)
    if transposed:
        both = jnp.concatenate([both, both], axis=1)
    total = jnp.zeros((8, TB), F32)
    for k in range(8):
        tile = split_ref[8 * g + k]
        if transposed:
            out = jnp.dot(both, tile, preferred_element_type=F32)
        else:
            out = lax.dot_general(both, tile, (((1,), (1,)), ((), ())), preferred_element_type=F32)
            out = out[:, :TB] + out[:, TB:]
        total = jnp.where(sub == k, out[:8] + out[8:], total)
    return jnp.where(live[8 * g : 8 * g + 8] > 0.0, total, 0.0)


def times_tiles(vectors, split_ref, live, transposed):
    groups = [times_group(g, vectors, split_ref, live, transposed) for g in range(CAP // 8)]
    return jnp.concatenate(groups, axis=0)


def split_tiles(tiles, split_ref, start, stop):
    for j in range(start, stop):
        high, low = two_parts(tiles[j])
        split_ref[j, :TB, :] = high.astype(BF16)
        split_ref[j, TB:, :] = low.astype(BF16)


def pick_rows(source, row_ref, picked):
    for j in range(CAP):
        picked[j : j + 1, :] = source[pl.ds(row_ref[j], 1), :]


def hits_of(wanted, lane_rows, width):
    pieces = [jnp.where(wanted == row, 1.0, 0.0) for row in lane_rows]
    return jnp.concatenate(pieces, axis=1)[:, :width].astype(BF16)


def index_row(index_ref, live, base):
    lane = iota((1, TB), 1)
    row = jnp.zeros((1, TB), F32)
    for j in range(CAP):
        value = jnp.where(j < live, index_ref[j] + 1, 0).astype(F32)
        row = jnp.where(lane == lax.rem(base + j, TB), value, row)
    return row


def index_lanes(in_ref, count):
    lane = iota((1, TB), 1)
    rows = []
    for k in range(-(-count * MSG // TB)):
        row = jnp.zeros((1, TB), F32)
        for i in range(count):
            low, high = MSG * i - TB * k, MSG * i + CAP - TB * k
            if high > 0 and low < TB:
                mine = (lane >= low) & (lane < high)
                row = jnp.where(mine, in_ref[MSG * i + CAP : MSG * (i + 1), :], row)
        rows.append(row)
    return rows


def send_to_all(out_ref, count, sums, row):
    message = jnp.concatenate([sums, row], axis=0)
    for i in range(count):
        out_ref[MSG * i : MSG * (i + 1), :] = message


def extra_sum(in_ref, count):
    row = in_ref[CAP : CAP + 1, :]
    for i in range(1, count):
        row = row + in_ref[MSG * i + CAP : MSG * (i + 1), :]
    return row


def scalar_row(rows):
    sums = jnp.sum(stack_rows(rows), axis=1, keepdims=True)
    apart = jnp.where(iota((EXTRA, TB), 0) == iota((EXTRA, TB), 1), sums, 0.0)
    return jnp.sum(apart, axis=0, keepdims=True)


def scalars_of(row, count):
    apart = jnp.where(iota((EXTRA, TB), 0) == iota((EXTRA, TB), 1), row, 0.0)
    sums = jnp.sum(apart, axis=1, keepdims=True)
    return [sums[k : k + 1] for k in range(count)]


def lane_sum(x):
    return jnp.sum(x, axis=0, keepdims=True)


def stack_rows(rows):
    sub = iota((EXTRA, TB), 0)
    out = jnp.zeros((EXTRA, TB), F32)
    for k, row in enumerate(rows):
        out = jnp.where(sub == k, row, out)
    return out


def first_kernel(
    row_hbm, col_hbm, live_hbm, tiles_hbm, scores_hbm, out_ref, info_ref,
    row_ref, col_ref, live_ref, tiles, scores, split_ref, picked, done,
):
    part = CAP // PARTS
    copies = [
        pltpu.make_async_copy(row_hbm, row_ref, done.at[0]),
        pltpu.make_async_copy(col_hbm, col_ref, done.at[1]),
        pltpu.make_async_copy(live_hbm, live_ref, done.at[2]),
        pltpu.make_async_copy(scores_hbm, scores, done.at[3]),
    ]
    for i in range(PARTS):
        some = pl.ds(part * i, part)
        copies.append(pltpu.make_async_copy(tiles_hbm.at[some], tiles.at[some], done.at[4 + i]))
    for copy in copies:
        copy.start()
    for copy in copies[:4]:
        copy.wait()
    live = live_ref[0]
    pick_rows(scores, row_ref, picked)
    far, _ = places()
    row = index_row(col_ref, live, far_slot(far) * MSG)
    sub = iota((CAP, TB), 0)
    mask = jnp.where(sub < live, 1.0, 0.0)
    own = jnp.full((CAP, TB), -1.0, F32)
    for j in range(CAP):
        own = jnp.where(sub == j, jnp.where(j < live, row_ref[j] + 1, -1).astype(F32), own)
    place = slot_of(lax.axis_index("cols"), COL_ORDER)
    info_ref[:CAP, :] = mask
    info_ref[CAP : 2 * CAP, :] = own
    info_ref[2 * CAP :, :] = stack_rows([index_row(row_ref, live, place * MSG)])
    groups, rows = [], picked[...]
    for i in range(PARTS):
        copies[4 + i].wait()
        split_tiles(tiles, split_ref, part * i, part * (i + 1))
        groups.append(times_group(i, rows, split_ref, mask, True))
    sums = jnp.concatenate(groups, axis=0)
    send_to_all(out_ref, FAR, sums, row)


def relay_kernel(in_ref, out_ref):
    rows = index_lanes(in_ref, FAR)
    for i in range(NEAR):
        out_ref[i] = in_ref[...]
        for k, row in enumerate(rows):
            out_ref[i, MSG * k + CAP : MSG * (k + 1), :] = row


def forward(vectors, split_ref, info_ref):
    return times_tiles(vectors[:CAP], split_ref, info_ref[:CAP, :], False)


def gathered_kernel(
    info_ref, in_ref, tiles_ref, out_ref, gradient_ref, hits_ref, split_ref, sums_ref
):
    split_tiles(tiles_ref, split_ref, 0, CAP)
    far, near = places()
    slot = far_slot(far)
    lines = -(-LINE // TB)
    index = [
        [in_ref[i, MSG * k + CAP : MSG * (k + 1), :] for k in range(lines)] for i in range(NEAR)
    ]
    own_rows = index[0]
    for i in range(1, NEAR):
        own_rows = [jnp.where(near == NEAR_ORDER[i], new, old) for new, old in zip(index[i], own_rows)]
    own_wanted = jnp.zeros((WANT, 1), F32)
    every_wanted = []
    lane, sub = iota((CAP, TB), 1), iota((CAP, TB), 0)
    for i in range(NEAR):
        found = jnp.zeros((CAP, TB), F32)
        for k in range(lines):
            found = jnp.where(lane + k * TB == sub + slot * MSG, index[i][k], found)
        tile_part = jnp.sum(found, axis=1, keepdims=True)
        tile_part = jnp.where(tile_part == 0.0, -1.0, tile_part)
        share_part = ((far * NEAR + NEAR_ORDER[i]) * SHARE + 1 + iota((SHARE, 1), 0)).astype(F32)
        wanted = jnp.concatenate([tile_part, share_part], axis=0)
        every_wanted.append(wanted)
        own_wanted = jnp.where(near == NEAR_ORDER[i], wanted, own_wanted)
    hits_ref[...] = hits_of(jnp.concatenate(every_wanted, axis=0), own_rows, LINE)
    gradient = jnp.zeros((WANT, TB), F32)
    for i in range(NEAR):
        gradient += picked_sum(hits_of(own_wanted, index[i], LINE), in_ref[i])
    gradient_ref[...] = gradient
    sums = forward(gradient, split_ref, info_ref)
    sums_ref[...] = sums
    send_to_all(out_ref, COLS, sums, info_ref[2 * CAP : 2 * CAP + 1, :])


def send_backward(picked, split_ref, info_ref, scalars, out_ref):
    sums = times_tiles(picked, split_ref, info_ref[:CAP, :], True)
    send_to_all(out_ref, FAR, sums, scalar_row(scalars))


def first_image_kernel(
    info_ref, in_ref, split_ref, scores_ref, out_ref, image_ref, hits_ref
):
    wanted = (iota((ROW_BLOCKS, 1), 0) + 1).astype(F32)
    wanted = jnp.concatenate([wanted, info_ref[CAP : 2 * CAP, :1]], axis=0)
    hits = hits_of(wanted, index_lanes(in_ref, COLS), SIDE)
    hits_ref[...] = hits
    sums = picked_sum(hits, in_ref[...])
    image = sums[:ROW_BLOCKS]
    image_ref[...] = image
    scalars = [lane_sum(image * scores_ref[...]), lane_sum(image * image)]
    send_backward(sums[ROW_BLOCKS:], split_ref, info_ref, scalars, out_ref)


def hand_kernel(in_ref, hits_ref, out_ref):
    extra = extra_sum(in_ref, FAR)
    sums = picked_sum(hits_ref[...], in_ref[...])
    for i in range(NEAR):
        some = jnp.concatenate([sums[WANT * i : WANT * (i + 1)], extra], axis=0)
        out_ref[HAND * i : HAND * (i + 1), :] = some


def added(in_ref):
    total = in_ref[:HAND, :]
    for i in range(1, NEAR):
        total = total + in_ref[HAND * i : HAND * (i + 1), :]
    return total


def second_gradient_kernel(
    info_ref, in_ref, split_ref, gradient_ref, sums_ref,
    out_ref, product_ref, next_ref, state_ref, product_sums_ref, next_sums_ref,
):
    total = added(in_ref)
    product = total[:WANT]
    product_sums = forward(product, split_ref, info_ref)
    product_sums_ref[...] = product_sums
    norm, image_norm = scalars_of(total[WANT : WANT + 1], 2)
    step = norm / image_norm
    following = gradient_ref[...] - step * product
    product_ref[...] = product
    next_ref[...] = following
    state_ref[...] = stack_rows([norm, image_norm, step])
    next_sums = sums_ref[...] - step * product_sums
    next_sums_ref[...] = next_sums
    send_to_all(out_ref, COLS, next_sums, jnp.zeros((1, TB), F32))


def second_image_kernel(
    info_ref, in_ref, split_ref, hits_ref, scores_ref, old_ref, state_ref, out_ref, image_ref
):
    sums = picked_sum(hits_ref[...], in_ref[...])
    image = sums[:ROW_BLOCKS]
    image_ref[...] = image
    old = old_ref[...]
    residual = scores_ref[...] - state_ref[2:3, :] * old
    scalars = [lane_sum(image * residual), lane_sum(image * image), lane_sum(image * old)]
    send_backward(sums[ROW_BLOCKS:], split_ref, info_ref, scalars, out_ref)


def third_gradient_kernel(
    info_ref, in_ref, split_ref, first_ref, second_ref, product_ref, state_ref,
    product_sums_ref, second_sums_ref, out_ref, keep_ref, later_ref,
):
    total = added(in_ref)
    product_sums = forward(total, split_ref, info_ref)
    old_norm, old_image_norm, old_step = state_ref[0:1, :], state_ref[1:2, :], state_ref[2:3, :]
    norm, straight, cross = scalars_of(total[WANT : WANT + 1], 3)
    ratio = norm / old_norm
    image_norm = straight + 2.0 * ratio * cross + ratio * ratio * old_image_norm
    step = norm / image_norm
    first, second = first_ref[...], second_ref[...]
    product = total[:WANT] + ratio * product_ref[...]
    third = second - step * product
    direction = second + ratio * first
    weights = old_step * first + step * direction
    keep_ref[0] = third[CAP:]
    keep_ref[1] = direction[CAP:]
    keep_ref[2] = weights[CAP:]
    later_ref[...] = stack_rows([norm, image_norm, step, ratio])
    product_sums = product_sums + ratio * product_sums_ref[...]
    send_to_all(out_ref, COLS, second_sums_ref[...] - step * product_sums, jnp.zeros((1, TB), F32))


def third_image_kernel(
    in_ref, hits_ref, scores_ref, first_ref, second_ref, state_ref, later_ref,
    out_ref, keep_ref,
):
    image = picked_sum(hits_ref[:ROW_BLOCKS, :], in_ref[...])
    first = first_ref[...]
    old = second_ref[...] + later_ref[3:4, :] * first
    residual = scores_ref[...] - state_ref[2:3, :] * first - later_ref[2:3, :] * old
    keep_ref[0] = image
    keep_ref[1] = old
    keep_ref[2] = residual
    scalars = [lane_sum(image * residual), lane_sum(image * image), lane_sum(image * old)]
    out_ref[...] = jnp.broadcast_to(scalar_row(scalars), (ROWS, TB))


def last_kernel(in_ref, keep_ref, image_ref, later_ref, weights_ref, residual_ref):
    norm, straight, cross = scalars_of(lane_sum(in_ref[...]), 3)
    ratio = norm / later_ref[0:1, :]
    image_norm = straight + 2.0 * ratio * cross + ratio * ratio * later_ref[1:2, :]
    step = norm / image_norm
    weights_ref[...] = keep_ref[2] + step * (keep_ref[0] + ratio * keep_ref[1])
    residual_ref[...] = image_ref[2] - step * (image_ref[0] + ratio * image_ref[1])


def call(kernel, outs, args, scratch=(), memory=None, room=16 * 2**20):
    def spec(x):
        scalar = x.dtype == jnp.int32
        return pl.BlockSpec(memory_space=memory or (pltpu.SMEM if scalar else pltpu.VMEM))

    return pl.pallas_call(
        kernel,
        out_shape=[jax.ShapeDtypeStruct(s, d) for s, d in outs],
        in_specs=[spec(a) for a in args],
        out_specs=[pl.BlockSpec(memory_space=pltpu.VMEM) for _ in outs],
        scratch_shapes=list(scratch),
        compiler_params=pltpu.CompilerParams(vmem_limit_bytes=room),
        name=kernel.__name__,
    )(*args)


GROUPS = {
    "far": [
        [(far * NEAR + near) * COLS + col for far in FAR_ORDERS[col % 2]]
        for near in range(NEAR)
        for col in range(COLS)
    ],
    "near": [[far * NEAR + near for near in NEAR_ORDER] for far in range(FAR)],
    "rows": [[far * NEAR + near for far in FAR_ORDERS[0] for near in NEAR_ORDER]],
    "cols": [COL_ORDER],
}


def swap(x, kind, count):
    shape = x.shape
    if shape == (count, TB):
        x = x.reshape(count * TB)
    elif len(shape) == 2:
        x = x.reshape(count, shape[0] // count, 1, TB)
    axis = {"cols": "cols", "far": ("rows", "cols")}.get(kind, "rows")
    groups = GROUPS[kind]
    return lax.all_to_all(x, axis, 0, 0, axis_index_groups=groups, tiled=True).reshape(shape)


def local(tiles, tile_row, tile_col, tile_counts, scores):
    f = lambda *shape: (shape, F32)
    b = lambda *shape: (shape, BF16)
    to_far, to_near = f(LINE, TB), f(NEAR * HAND, TB)
    to_cols = f(SIDE, TB)
    own = f(CAP, TB)
    image_shape, state_shape = f(ROW_BLOCKS, TB), f(EXTRA, TB)

    message, info = call(
        first_kernel,
        [to_far, f(INFO, TB)],
        [tile_row, tile_col, tile_counts, tiles, scores],
        [
            pltpu.SMEM((CAP,), jnp.int32),
            pltpu.SMEM((CAP,), jnp.int32),
            pltpu.SMEM((1,), jnp.int32),
            pltpu.VMEM((CAP, TB, TB), F32),
            pltpu.VMEM((ROW_BLOCKS, TB), F32),
            pltpu.VMEM((CAP, 2 * TB, TB), BF16),
            pltpu.VMEM((CAP, TB), F32),
            pltpu.SemaphoreType.DMA((4 + PARTS,)),
        ],
        pltpu.HBM,
        62 * 2**20,
    )
    (message,) = call(relay_kernel, [f(NEAR, LINE, TB)], [swap(message, "far", FAR)])
    message, first, hand_hits, split, first_sums = call(
        gathered_kernel,
        [to_cols, f(WANT, TB), b(NEAR * WANT, LINE), b(CAP, 2 * TB, TB), own],
        [info, swap(message, "near", NEAR), tiles],
    )
    message, image, row_hits = call(
        first_image_kernel,
        [to_far, image_shape, b(ROW_BLOCKS + CAP, SIDE)],
        [info, swap(message, "cols", COLS), split, scores],
    )
    (message,) = call(hand_kernel, [to_near], [swap(message, "far", FAR), hand_hits])
    message, product, second, state, product_sums, second_sums = call(
        second_gradient_kernel,
        [to_cols, f(WANT, TB), f(WANT, TB), state_shape, own, own],
        [info, swap(message, "near", NEAR), split, first, first_sums],
    )
    message, second_image = call(
        second_image_kernel,
        [to_far, image_shape],
        [info, swap(message, "cols", COLS), split, row_hits, scores, image, state],
    )
    (message,) = call(hand_kernel, [to_near], [swap(message, "far", FAR), hand_hits])
    message, keep, later = call(
        third_gradient_kernel,
        [to_cols, f(3, SHARE, TB), state_shape],
        [
            info, swap(message, "near", NEAR), split, first, second, product, state,
            product_sums, second_sums,
        ],
    )
    message, images = call(
        third_image_kernel,
        [f(ROWS, TB), f(3, ROW_BLOCKS, TB)],
        [swap(message, "cols", COLS), row_hits, scores, image, second_image, state, later],
    )
    weights, residual = call(
        last_kernel,
        [f(SHARE, TB), image_shape],
        [swap(message, "rows", ROWS), keep, images, later],
    )
    return weights, residual


def solution(mesh):
    every = ("rows", "cols")
    return jax.shard_map(
        local,
        mesh=mesh,
        in_specs=(P(every, None, None), P(every), P(every), P(every), P("rows", None)),
        out_specs=(P(("cols", "rows"), None), P("rows", None)),
        check_vma=False,
    )
```
